32 devices in a mesh: dp: 4 (over y, x), proto: 8 (over z, core).
Axes of the slice: x: 2, y: 2, z: 4, core: 2. Of those that a mesh axis runs over, the one named last changes fastest.
Arguments:
- first_view: bfloat16 [2048, 128], P('dp'), may hold values from -6 to 6
- alternate_augmentation: bfloat16 [2048, 128], P('dp'), may hold values from -6 to 6
- prototypes: bfloat16 [32768, 128], P('proto'), may hold values from -6 to 6
Outputs:
- proto_grad: float32 [32768, 128], P('proto')
- token_grad: float32 [2048, 128], P('dp')
The draws below stay inside these ranges and needn't reach their ends.
All inputs are finite; a program needn't handle non-finite values.
Results may differ from the reference program's by a relative error of at most 0.0003.
The reference program's roundings to bfloat16 on the way count: a program that leaves them out, or rounds other values in their place, can miss the bound.
Values may be sent and summed in bfloat16 or wider, within the bound.
No kernel may reach another device: no remote copies, remote signals or barrier semaphores. Data moves between devices by JAX's collectives and lax.ppermute only.
A program may use at most 64 MiB of HBM per device.

```python
import jax
import jax.numpy as jnp
from jax import lax

D = 128
PROTO_DEV = 4096
PROTOS = 32768
TOKENS = 2048
BALANCING_PASSES = 3
N_PROTO = 8


def level_of(own_key, dims, split, least, high):
    factor_of, own = 1.0, jax.random.fold_in(own_key, 6)
    for position, parts in split:
        heights = jnp.exp(jax.random.uniform(jax.random.fold_in(own, position), (parts,), jnp.float32, least / len(split), high / len(split)))
        factor_of = factor_of * jnp.repeat(heights, dims[position] // parts).reshape([-1 if axis == position else 1 for axis in range(len(dims))])
    return factor_of


def normal_values(stream_key, dims, spread, most, cuts=(), kind=jnp.bfloat16):
    level = level_of(stream_key, dims, cuts, -0.22, 0.18) if cuts else 1.0
    entries = jax.random.normal(stream_key, dims, jnp.float32) * spread * level
    return jnp.minimum(jnp.maximum(entries, -most), most).astype(kind)


def setup_inputs(seed: int = 0) -> dict:
    key_of = jax.random.split(jax.random.key(seed), 4)
    return {
        "first_view": normal_values(key_of[0], (TOKENS, D), 1.0, 6.0, ((0, 4),)),
        "alternate_augmentation": normal_values(key_of[1], (TOKENS, D), 1.0, 6.0, ((0, 4),)),
        "prototypes": normal_values(key_of[2], (PROTOS, D), 1.0, 6.0, ((0, 8),)),
    }


CODE_TEMP = 0.05
PRED_TEMP = 0.1

def normalize(values):
    floats = values.astype(jnp.float32)
    mean_square = lax.optimization_barrier(jnp.mean(floats * floats, axis=-1, keepdims=True))
    inverse_root = lax.rsqrt(mean_square + 1e-06)
    return (floats * inverse_root).astype(jnp.bfloat16)

def exponential_piece(row_slice, centroid_block, softness_level):
    return jnp.exp(jnp.dot(row_slice, centroid_block.T, preferred_element_type=jnp.float32) / row_slice.shape[1] / softness_level)

def logit_grads(anchors, soft_labels, token_scale, divisor_value, centroid_block, cluster_center_factor, proto_total):
    assigned = exponential_piece(anchors, centroid_block, CODE_TEMP) * cluster_center_factor[None, :] * token_scale[:, None]
    predicted = exponential_piece(soft_labels, centroid_block, PRED_TEMP) / divisor_value[:, None]
    return (proto_total * (predicted - assigned)).astype(jnp.bfloat16)

def reference(first_view, alternate_augmentation, prototypes):
    anchors = normalize(first_view)
    soft_labels = normalize(alternate_augmentation)
    centres = normalize(prototypes).reshape(N_PROTO, PROTO_DEV, D)
    token_scale = jnp.ones((TOKENS,), jnp.float32)
    cluster_center_factor = jnp.ones((N_PROTO, PROTO_DEV), jnp.float32)
    for iteration_number in range(BALANCING_PASSES):
        current = token_scale
        prototype_marginals = lax.map(lambda centroid_block: lax.optimization_barrier(jnp.sum(exponential_piece(anchors, centroid_block, CODE_TEMP) * current[:, None], axis=0)), centres)
        cluster_center_factor = 1.0 / (PROTOS * prototype_marginals)
        row_parts = lax.map(lambda packed: lax.optimization_barrier(jnp.sum(exponential_piece(anchors, packed[0], CODE_TEMP) * packed[1][None, :], axis=1)), (centres, cluster_center_factor))
        token_scale = 1.0 / lax.optimization_barrier(jnp.sum(row_parts, axis=0))
    divisor_value = lax.optimization_barrier(jnp.sum(lax.map(lambda centroid_block: lax.optimization_barrier(jnp.sum(exponential_piece(soft_labels, centroid_block, PRED_TEMP), axis=1)), centres), axis=0))

    def final_tile(running_total, packed):
        centroid_block, block_scale = packed
        logit_grad = logit_grads(anchors, soft_labels, token_scale, divisor_value, centroid_block, block_scale, PROTOS)
        proto_part = jnp.dot(logit_grad.T, soft_labels, preferred_element_type=jnp.float32)
        return (running_total + jnp.dot(logit_grad, centroid_block, preferred_element_type=jnp.float32), proto_part)
    token_sum, proto_parts = lax.scan(final_tile, jnp.zeros((TOKENS, D), jnp.float32), (centres, cluster_center_factor))
    return (proto_parts.reshape(PROTOS, D) * TOKENS ** (-0.5), token_sum * PROTOS ** (-0.5))
```

```python
import functools
import math

import jax
import jax.numpy as jnp
from jax import lax
from jax.experimental import pallas as pl
from jax.experimental.pallas import tpu as pltpu
from jax.sharding import PartitionSpec as P

CODE_TEMP = 0.05
PRED_TEMP = 0.1
F32 = jnp.float32
BF16 = jnp.bfloat16
VMEM_LIMIT = 20 << 20


def vmem_spec():
    return pl.BlockSpec(memory_space=pltpu.VMEM)


def shape(*dims, dtype=F32):
    return jax.ShapeDtypeStruct(dims, dtype)


def normalize(values):
    floats = values.astype(F32)
    mean_square = jnp.mean(floats * floats, axis=-1, keepdims=True)
    return (floats * lax.rsqrt(mean_square + 1e-06)).astype(BF16)


def rows(i, size):
    return pl.ds(pl.multiple_of(i * size, size), size)


def similarity(a, b):
    return lax.dot_general(a, b, (((1,), (1,)), ((), ())), preferred_element_type=F32)


def sublane_sums(block):
    return jnp.sum(block.reshape(block.shape[0] // 8, 8, block.shape[1]), axis=0)


def first_pass(*refs, parts, block, scale, total):
    proto_ref, token_refs = refs[0], refs[1 : 1 + parts]
    code_ref, centre_ref, out_ref, tok, acc = refs[1 + parts :]
    n = token_refs[0].shape[0]
    for i, t in enumerate(token_refs):
        tok[i * n : (i + 1) * n, :] = normalize(t[...])
    acc[...] = jnp.zeros_like(acc)

    def step(i, carry):
        at = rows(i, block)
        centre = normalize(proto_ref[at, :])
        centre_ref[at, :] = centre
        code = jnp.exp2(similarity(centre, tok[...]) * scale)
        code_ref[at, :] = code
        factor = 1.0 / (total * jnp.sum(code, axis=1, keepdims=True))
        acc[...] += sublane_sums(code * factor)
        return carry

    lax.fori_loop(0, proto_ref.shape[0] // block, step, 0)
    out_ref[...] = jnp.sum(acc[...], axis=0, keepdims=True)


def denominators(*refs, parts, block, scale):
    centre_ref, token_refs = refs[0], refs[1 : 1 + parts]
    tok, out_ref, acc = refs[1 + parts :]
    n = token_refs[0].shape[0]
    for i, t in enumerate(token_refs):
        tok[i * n : (i + 1) * n, :] = normalize(t[...])
    acc[...] = jnp.zeros_like(acc)

    def step(i, carry):
        centre = centre_ref[rows(i, block), :]
        acc[...] += sublane_sums(jnp.exp2(similarity(centre, tok[...]) * scale))
        return carry

    lax.fori_loop(0, centre_ref.shape[0] // block, step, 0)
    out_ref[...] = jnp.sum(acc[...], axis=0, keepdims=True)


def middle_pass(*refs, parts, block, total, extra):
    code_ref, sum_refs = refs[0], refs[1 : 1 + parts]
    if extra:
        extra_ref, out_ref, factor_ref, acc = refs[1 + parts :]
    else:
        out_ref, factor_ref, acc = refs[1 + parts :]
    sums = sum_refs[0][0:1, :]
    for s in sum_refs[1:]:
        sums = sums + s[0:1, :]
    token_scale = 1.0 / sums
    acc[...] = jnp.zeros_like(acc)

    def step(i, carry):
        at = rows(i, block)
        code = code_ref[at, :]
        factor = 1.0 / (total * jnp.sum(code * token_scale, axis=1, keepdims=True))
        factor_ref[at, :] = factor
        acc[...] += sublane_sums(code * factor)
        return carry

    lax.fori_loop(0, code_ref.shape[0] // block, step, 0)
    out_ref[0:1, :] = jnp.sum(acc[...], axis=0, keepdims=True)
    if extra:
        out_ref[1:2, :] = extra_ref[...]


def token_part(*refs, parts, block, scale, total, own):
    code_ref, centre_ref, tok_ref, factor_ref = refs[:4]
    sum_refs, den_refs = refs[4 : 4 + parts], refs[4 + parts : 4 + 2 * parts]
    grad_ref, logit_ref, scales_ref, acc = refs[4 + 2 * parts :]
    sums, den = sum_refs[0][0:1, :], den_refs[0][1:2, :]
    for s in sum_refs[1:]:
        sums = sums + s[0:1, :]
    for d in den_refs[1:]:
        den = den + d[1:2, :]
    scales_ref[0:1, :] = total / sums
    scales_ref[1:2, :] = total / den
    acc[...] = jnp.zeros_like(acc)
    token_scale, weight = scales_ref[0:1, :own], scales_ref[1:2, :own]

    def step(i, carry):
        at = rows(i, block)
        centre = centre_ref[at, :]
        pred = jnp.exp2(similarity(centre, tok_ref[:own, :]) * scale)
        code = code_ref[at, :own]
        logit = (pred * weight - code * factor_ref[at, :] * token_scale).astype(BF16)
        logit_ref[at, :] = logit
        acc[...] += lax.dot_general(
            centre, logit, (((0,), (0,)), ((), ())), preferred_element_type=F32
        )
        return carry

    lax.fori_loop(0, code_ref.shape[0] // block, step, 0)
    grad_ref[...] = acc[...].T * total ** (-0.5)


def proto_part(
    code_ref, centre_ref, tok_ref, factor_ref, scales_ref, logit_ref, out_ref, *, block, scale, own
):
    tokens = code_ref.shape[1]
    token_scale, weight = scales_ref[0:1, own:], scales_ref[1:2, own:]

    def step(i, carry):
        at = rows(i, block)
        pred = jnp.exp2(similarity(centre_ref[at, :], tok_ref[own:, :]) * scale)
        code = code_ref[at, own:]
        logit = (pred * weight - code * factor_ref[at, :] * token_scale).astype(BF16)
        grad = jnp.dot(logit, tok_ref[own:, :], preferred_element_type=F32)
        grad += jnp.dot(logit_ref[at, :], tok_ref[:own, :], preferred_element_type=F32)
        out_ref[at, :] = grad * tokens ** (-0.5)
        return carry

    lax.fori_loop(0, code_ref.shape[0] // block, step, 0)


def shifted(x, axis):
    n = lax.axis_size(axis)
    return [x] + [
        lax.ppermute(x, axis, [(i, (i + s) % n) for i in range(n)]) for s in range(1, n)
    ]


def swapped(x, axis, mask):
    return lax.ppermute(x, axis, [(i, i ^ mask) for i in range(lax.axis_size(axis))])


def proto_terms(x):
    n = lax.axis_size("proto")
    x = x + swapped(x, "proto", 1)
    terms, unit = [x], 2
    while unit < n:
        group = min(4, n // unit)
        if unit > 2:
            terms = [sum(terms)]
        terms = [terms[0]] + [swapped(terms[0], "proto", unit * m) for m in range(1, group)]
        unit *= group
    return terms


def proto_sum(x):
    n = lax.axis_size("proto")
    core = lax.rem(lax.axis_index("proto"), 2)
    half = x.shape[0] // 2
    mine = lax.dynamic_slice_in_dim(x, core * half, half)
    other = lax.dynamic_slice_in_dim(x, (1 - core) * half, half)
    mine = mine + swapped(other, "proto", 1)
    unit = 2
    while unit < n:
        group = min(4, n // unit)
        mine = sum([swapped(mine, "proto", unit * m) for m in range(1, group)], mine)
        unit *= group
    other = swapped(mine, "proto", 1)
    return jnp.where(
        core == 0, jnp.concatenate([mine, other]), jnp.concatenate([other, mine])
    )


def local(first_view, alternate_augmentation, prototypes):
    own, d = first_view.shape
    k = prototypes.shape[0]
    tokens = own * lax.axis_size("dp")
    total = float(k * lax.axis_size("proto"))
    log2e = math.log2(math.e)
    code_scale = log2e / d / CODE_TEMP
    pred_scale = log2e / d / PRED_TEMP
    views = shifted(first_view, "dp")
    others = shifted(alternate_augmentation, "dp")
    dp = len(views)
    block = min(512, k)

    def run(body, outs, args, scratch, resident=(), keep=(), us=1.0):
        shapes = tuple(pltpu.VMEM(s.shape, s.dtype) if i in keep else s for i, s in enumerate(outs))
        args = [
            pltpu.with_memory_space_constraint(a, pltpu.VMEM) if i in resident else a
            for i, a in enumerate(args)
        ]
        return pl.pallas_call(
            body,
            out_shape=shapes,
            in_specs=[vmem_spec()] * len(args),
            out_specs=tuple(vmem_spec() for _ in outs),
            scratch_shapes=scratch,
            compiler_params=pltpu.CompilerParams(vmem_limit_bytes=VMEM_LIMIT),
            cost_estimate=pl.CostEstimate(
                flops=int(us * 1e9), bytes_accessed=1 << 20, transcendentals=0
            ),
        )(*args)

    acc = pltpu.VMEM((8, tokens), F32)
    code, centres, sums = run(
        functools.partial(first_pass, parts=dp, block=block, scale=code_scale, total=total),
        [shape(k, tokens), shape(k, d, dtype=BF16), shape(1, tokens)],
        [prototypes] + views,
        [pltpu.VMEM((tokens, d), BF16), acc],
        keep=(0, 1),
        us=8,
    )
    terms = proto_terms(sums)
    tok, den = run(
        functools.partial(denominators, parts=dp, block=block, scale=pred_scale),
        [shape(tokens, d, dtype=BF16), shape(1, tokens)],
        [centres] + others,
        [acc],
        resident=(0,),
        keep=(0,),
        us=6,
    )
    sums, _ = run(
        functools.partial(middle_pass, parts=len(terms), block=block, total=total, extra=True),
        [shape(2, tokens), shape(k, 1)],
        [code] + terms + [den],
        [acc],
        resident=(0,),
        keep=(1,),
        us=5,
    )
    den_terms = proto_terms(sums)
    sums, factor = run(
        functools.partial(
            middle_pass, parts=len(den_terms), block=block, total=total, extra=False
        ),
        [shape(1, tokens), shape(k, 1)],
        [code] + den_terms,
        [acc],
        resident=(0,),
        keep=(1,),
        us=5,
    )
    terms = proto_terms(sums)
    token_grad, logit, scales = run(
        functools.partial(
            token_part, parts=len(terms), block=block, scale=pred_scale, total=total, own=own
        ),
        [shape(own, d), shape(k, own, dtype=BF16), shape(2, tokens)],
        [code, centres, tok, factor] + terms + den_terms,
        [pltpu.VMEM((d, own), F32)],
        resident=(0, 1, 2, 3),
        keep=(1, 2),
        us=4,
    )
    (proto_grad,) = run(
        functools.partial(proto_part, block=block, scale=pred_scale, own=own),
        [shape(k, d)],
        [code, centres, tok, factor, scales, logit],
        [],
        resident=(0, 1, 2, 3, 4, 5),
        us=10,
    )
    return proto_grad, proto_sum(token_grad)


def solution(mesh):
    return jax.shard_map(
        local,
        mesh=mesh,
        in_specs=(P("dp", None), P("dp", None), P("proto", None)),
        out_specs=(P("proto", None), P("dp", None)),
        check_vma=False,
    )
```

```python
import functools
import math

import jax
import jax.numpy as jnp
from jax import lax
from jax.experimental import pallas as pl
from jax.experimental.pallas import tpu as pltpu
from jax.sharding import PartitionSpec as P

CODE_TEMP = 0.05
PRED_TEMP = 0.1
F32 = jnp.float32
BF16 = jnp.bfloat16
VMEM_LIMIT = 24 << 20


def vmem_spec():
    return pl.BlockSpec(memory_space=pltpu.VMEM)


def shape(*dims, dtype=F32):
    return jax.ShapeDtypeStruct(dims, dtype)


def normalize(values):
    floats = values.astype(F32)
    mean_square = jnp.mean(floats * floats, axis=-1, keepdims=True)
    return (floats * lax.rsqrt(mean_square + 1e-06)).astype(BF16)


def rows(i, size):
    return pl.ds(pl.multiple_of(i * size, size), size)


def similarity(a, b):
    return lax.dot_general(a, b, (((1,), (1,)), ((), ())), preferred_element_type=F32)


def sublane_sums(block):
    return jnp.sum(block.reshape(block.shape[0] // 8, 8, block.shape[1]), axis=0)


def first_pass(*refs, parts, block, scale, total):
    proto_ref, token_refs = refs[0], refs[1 : 1 + parts]
    code_ref, centre_ref, out_ref, tok, acc = refs[1 + parts :]
    n = token_refs[0].shape[0]
    for i, t in enumerate(token_refs):
        tok[i * n : (i + 1) * n, :] = normalize(t[...])
    acc[...] = jnp.zeros_like(acc)

    def step(i, carry):
        at = rows(i, block)
        centre = normalize(proto_ref[at, :])
        centre_ref[at, :] = centre
        code = jnp.exp2(similarity(centre, tok[...]) * scale)
        code_ref[at, :] = code
        factor = 1.0 / (total * jnp.sum(code, axis=1, keepdims=True))
        acc[...] += sublane_sums(code * factor)
        return carry

    lax.fori_loop(0, proto_ref.shape[0] // block, step, 0)
    out_ref[...] = jnp.sum(acc[...], axis=0, keepdims=True)


def denominators(*refs, parts, block, scale):
    centre_ref, token_refs = refs[1], refs[2 : 2 + parts]
    _, tok, out_ref, acc = refs[2 + parts :]
    n = token_refs[0].shape[0]
    for i, t in enumerate(token_refs):
        tok[i * n : (i + 1) * n, :] = normalize(t[...])
    acc[...] = jnp.zeros_like(acc)

    def step(i, carry):
        centre = centre_ref[rows(i, block), :]
        acc[...] += sublane_sums(jnp.exp2(similarity(centre, tok[...]) * scale))
        return carry

    lax.fori_loop(0, centre_ref.shape[0] // block, step, 0)
    out_ref[...] = jnp.sum(acc[...], axis=0, keepdims=True)


def middle_pass(*refs, parts, block, total, extra):
    code_ref, sum_refs = refs[0], refs[1 : 1 + parts]
    if extra:
        extra_ref, _, out_ref, factor_ref, acc = refs[1 + parts :]
    else:
        _, out_ref, factor_ref, acc = refs[1 + parts :]
    sums = sum_refs[0][0:1, :]
    for s in sum_refs[1:]:
        sums = sums + s[0:1, :]
    token_scale = 1.0 / sums
    acc[...] = jnp.zeros_like(acc)

    def step(i, carry):
        at = rows(i, block)
        code = code_ref[at, :]
        factor = 1.0 / (total * jnp.sum(code * token_scale, axis=1, keepdims=True))
        factor_ref[at, :] = factor
        acc[...] += sublane_sums(code * factor)
        return carry

    lax.fori_loop(0, code_ref.shape[0] // block, step, 0)
    out_ref[0:1, :] = jnp.sum(acc[...], axis=0, keepdims=True)
    if extra:
        out_ref[1:2, :] = extra_ref[...]


def token_part(*refs, parts, block, scale, total, own):
    code_ref, centre_ref, tok_ref, factor_ref = refs[:4]
    core = lax.rem(lax.axis_index("proto"), 2)
    sum_refs, den_refs = refs[4 : 4 + parts], refs[4 + parts : 4 + 2 * parts]
    _, mine_ref, other_ref, scales_ref, acc = refs[4 + 2 * parts :]
    sums, den = sum_refs[0][0:1, :], den_refs[0][1:2, :]
    for s in sum_refs[1:]:
        sums = sums + s[0:1, :]
    for d in den_refs[1:]:
        den = den + d[1:2, :]
    scales_ref[0:1, :] = total / sums
    scales_ref[1:2, :] = total / den
    acc[...] = jnp.zeros_like(acc)
    token_scale, weight = scales_ref[0:1, :own], scales_ref[1:2, :own]

    def step(i, carry):
        at = rows(i, block)
        centre = centre_ref[at, :]
        pred = jnp.exp2(similarity(centre, tok_ref[:own, :]) * scale)
        code = code_ref[at, :own]
        logit = (pred * weight - code * factor_ref[at, :] * token_scale).astype(BF16)
        acc[...] += lax.dot_general(
            centre, logit, (((0,), (0,)), ((), ())), preferred_element_type=F32
        )
        return carry

    lax.fori_loop(0, code_ref.shape[0] // block, step, 0)
    acc[...] = acc[...] * total ** (-0.5)
    half = own // 2
    for c in range(2):

        @pl.when(core == c)
        def _():
            mine_ref[...] = acc[:, c * half : (c + 1) * half].T
            other_ref[...] = acc[:, (1 - c) * half : (2 - c) * half].T


def proto_part(code_ref, centre_ref, tok_ref, factor_ref, scales_ref, out_ref, *, block, scale):
    tokens = code_ref.shape[1]
    token_scale, weight = scales_ref[0:1, :], scales_ref[1:2, :]

    def step(i, carry):
        at = rows(i, block)
        pred = jnp.exp2(similarity(centre_ref[at, :], tok_ref[...]) * scale)
        logit = (pred * weight - code_ref[at, :] * factor_ref[at, :] * token_scale).astype(BF16)
        grad = jnp.dot(logit, tok_ref[...], preferred_element_type=F32)
        out_ref[at, :] = grad * tokens ** (-0.5)
        return carry

    lax.fori_loop(0, code_ref.shape[0] // block, step, 0)


def shifted(x, axis):
    n = lax.axis_size(axis)
    return [x] + [
        lax.ppermute(x, axis, [(i, (i + s) % n) for i in range(n)]) for s in range(1, n)
    ]


def swapped(x, axis, mask):
    return lax.ppermute(x, axis, [(i, i ^ mask) for i in range(lax.axis_size(axis))])


def proto_terms(x):
    n = lax.axis_size("proto")
    x = x + swapped(x, "proto", 1)
    terms, unit = [x], 2
    while unit < n:
        group = min(4, n // unit)
        if unit > 2:
            terms = [sum(terms)]
        terms = [terms[0]] + [swapped(terms[0], "proto", unit * m) for m in range(1, group)]
        unit *= group
    return terms


def chip_sum(x):
    n, unit = lax.axis_size("proto"), 2
    while unit < n:
        group = min(4, n // unit)
        x = sum([swapped(x, "proto", unit * m) for m in range(1, group)], x)
        unit *= group
    return x


def local(first_view, alternate_augmentation, prototypes):
    own, d = first_view.shape
    k = prototypes.shape[0]
    tokens = own * lax.axis_size("dp")
    total = float(k * lax.axis_size("proto"))
    log2e = math.log2(math.e)
    code_scale = log2e / d / CODE_TEMP
    pred_scale = log2e / d / PRED_TEMP
    views = shifted(first_view, "dp")
    others = shifted(alternate_augmentation, "dp")
    dp = len(views)
    block = min(512, k)

    def run(body, outs, args, scratch, resident=(), keep=(), us=1.0, thread=False):
        if thread:
            outs, keep = [shape(*args[0].shape, dtype=args[0].dtype)] + outs, [0] + [i + 1 for i in keep]
        shapes = tuple(pltpu.VMEM(s.shape, s.dtype) if i in keep else s for i, s in enumerate(outs))
        args = [
            pltpu.with_memory_space_constraint(a, pltpu.VMEM) if i in resident else a
            for i, a in enumerate(args)
        ]
        return pl.pallas_call(
            body,
            out_shape=shapes,
            in_specs=[vmem_spec()] * len(args),
            out_specs=tuple(vmem_spec() for _ in outs),
            scratch_shapes=scratch,
            input_output_aliases={0: 0} if thread else {},
            compiler_params=pltpu.CompilerParams(vmem_limit_bytes=VMEM_LIMIT),
            cost_estimate=pl.CostEstimate(
                flops=int(us * 1e9), bytes_accessed=1 << 20, transcendentals=0
            ),
        )(*args)

    acc = pltpu.VMEM((8, tokens), F32)
    code, centres, sums = run(
        functools.partial(first_pass, parts=dp, block=block, scale=code_scale, total=total),
        [shape(k, tokens), shape(k, d, dtype=BF16), shape(1, tokens)],
        [prototypes] + views,
        [pltpu.VMEM((tokens, d), BF16), acc],
        keep=(0, 1),
        us=8,
    )
    terms = proto_terms(sums)
    code, tok, den = run(
        functools.partial(denominators, parts=dp, block=block, scale=pred_scale),
        [shape(tokens, d, dtype=BF16), shape(1, tokens)],
        [code, centres] + others,
        [acc],
        resident=(0, 1),
        keep=(0,),
        thread=True,
        us=6,
    )
    code, sums, _ = run(
        functools.partial(middle_pass, parts=len(terms), block=block, total=total, extra=True),
        [shape(2, tokens), shape(k, 1)],
        [code] + terms + [den],
        [acc],
        resident=(0,),
        keep=(1,),
        thread=True,
        us=5,
    )
    den_terms = proto_terms(sums)
    code, sums, factor = run(
        functools.partial(
            middle_pass, parts=len(den_terms), block=block, total=total, extra=False
        ),
        [shape(1, tokens), shape(k, 1)],
        [code] + den_terms,
        [acc],
        resident=(0,),
        keep=(1,),
        thread=True,
        us=5,
    )
    terms = proto_terms(sums)
    code, mine, other, scales = run(
        functools.partial(
            token_part, parts=len(terms), block=block, scale=pred_scale, total=total, own=own
        ),
        [shape(own // 2, d), shape(own // 2, d), shape(2, tokens)],
        [code, centres, tok, factor] + terms + den_terms,
        [pltpu.VMEM((d, own), F32)],
        resident=(0, 1, 2, 3),
        keep=(2,),
        thread=True,
        us=4,
    )
    mine = chip_sum(mine + swapped(other, "proto", 1))
    (proto_grad,) = run(
        functools.partial(proto_part, block=block, scale=pred_scale),
        [shape(k, d)],
        [code, centres, tok, factor, scales],
        [],
        resident=(0, 1, 2, 3, 4),
        us=10,
    )
    mine, proto_grad = lax.optimization_barrier((mine, proto_grad))
    other = swapped(mine, "proto", 1)
    first = lax.rem(lax.axis_index("proto"), 2) == 0
    token_grad = jnp.where(
        first, jnp.concatenate([mine, other]), jnp.concatenate([other, mine])
    )
    return proto_grad, token_grad


def solution(mesh):
    return jax.shard_map(
        local,
        mesh=mesh,
        in_specs=(P("dp", None), P("dp", None), P("proto", None)),
        out_specs=(P("proto", None), P("dp", None)),
        check_vma=False,
    )
```

```python
import functools
import math

import jax
import jax.numpy as jnp
from jax import lax
from jax.experimental import pallas as pl
from jax.experimental.pallas import tpu as pltpu
from jax.sharding import PartitionSpec as P

CODE_TEMP = 0.05
PRED_TEMP = 0.1
F32 = jnp.float32
BF16 = jnp.bfloat16
VMEM_LIMIT = 20 << 20
BLOCKS = {"own": 1024, "first": 512, "den": 512, "middle": 512, "token": 1024, "proto": 512}


def vmem_spec():
    return pl.BlockSpec(memory_space=pltpu.VMEM)


def shape(*dims, dtype=F32):
    return jax.ShapeDtypeStruct(dims, dtype)


def run(body, outs, args, scratch, resident=(), keep=(), us=1.0, thread=False):
    if thread:
        outs = [shape(*args[0].shape, dtype=args[0].dtype)] + outs
        keep = [0] + [i + 1 for i in keep]
        resident = [0] + list(resident)
    return pl.pallas_call(
        body,
        out_shape=tuple(pltpu.VMEM(s.shape, s.dtype) if i in keep else s for i, s in enumerate(outs)),
        in_specs=[vmem_spec()] * len(args),
        out_specs=tuple(vmem_spec() for _ in outs),
        scratch_shapes=scratch,
        input_output_aliases={0: 0} if thread else {},
        compiler_params=pltpu.CompilerParams(vmem_limit_bytes=VMEM_LIMIT),
        cost_estimate=pl.CostEstimate(flops=int(us * 1e9), bytes_accessed=1 << 20, transcendentals=0),
    )(
        *[
            pltpu.with_memory_space_constraint(a, pltpu.VMEM) if i in resident else a
            for i, a in enumerate(args)
        ]
    )


def normalize(values):
    floats = values.astype(F32)
    mean_square = jnp.mean(floats * floats, axis=-1, keepdims=True)
    return (floats * lax.rsqrt(mean_square + 1e-06)).astype(BF16)


def steps(name, size, step):
    block = min(BLOCKS[name], size)

    def body(i, carry):
        step(pl.ds(pl.multiple_of(i * block, block), block))
        return carry

    lax.fori_loop(0, size // block, body, 0)


def similarity(a, b):
    return lax.dot_general(a, b, (((1,), (1,)), ((), ())), preferred_element_type=F32)


def sublane_sums(block):
    return jnp.sum(block.reshape(block.shape[0] // 8, 8, block.shape[1]), axis=0)


def own_codes(proto_ref, token_ref, code_ref, centre_ref, column_ref, *, scale):
    own = token_ref.shape[0]
    tok = normalize(token_ref[...])

    def step(at):
        centre = normalize(proto_ref[at, :])
        centre_ref[at, :] = centre
        code = jnp.exp2(similarity(centre, tok) * scale)
        code_ref[at, :own] = code
        column_ref[at, :] = jnp.sum(code, axis=1, keepdims=True)

    steps("own", proto_ref.shape[0], step)


def first_pass(*refs, parts, scale, total):
    (own_ref, centre_ref, column_ref), token_refs = refs[:3], refs[3 : 3 + parts]
    code_ref, out_ref, tok, acc = refs[3 + parts :]
    n = token_refs[0].shape[0]
    for i, t in enumerate(token_refs):
        tok[i * n : (i + 1) * n, :] = normalize(t[...])
    acc[...] = jnp.zeros_like(acc)

    def step(at):
        code = jnp.exp2(similarity(centre_ref[at, :], tok[...]) * scale)
        code_ref[at, n:] = code
        factor = 1.0 / (total * (column_ref[at, :] + jnp.sum(code, axis=1, keepdims=True)))
        acc[:, n:] += sublane_sums(code * factor)
        acc[:, :n] += sublane_sums(own_ref[at, :n] * factor)

    steps("first", centre_ref.shape[0], step)
    out_ref[...] = jnp.sum(acc[...], axis=0, keepdims=True)


def denominators(code_in, centre_ref, tok_ref, code_ref, out_ref, acc, *, scale, first, last):
    acc[...] = jnp.zeros_like(acc)
    block = min(BLOCKS["den"], centre_ref.shape[0] // 2)
    tok = tok_ref[...]

    def body(i, carry):
        centre = centre_ref[pl.ds(pl.multiple_of(i * block, block), block), :]
        acc[...] += sublane_sums(jnp.exp2(similarity(centre, tok) * scale))
        return carry

    lax.fori_loop(first // block, last // block, body, 0)
    out_ref[...] = jnp.sum(acc[...], axis=0, keepdims=True)


def target_rows(code_in, *refs):
    *token_refs, code_ref, tok = refs
    n = token_refs[0].shape[0]
    for i, t in enumerate(token_refs):
        tok[i * n : (i + 1) * n, :] = normalize(t[...])


def middle_pass(*refs, parts, extras, total):
    code_ref, sum_refs, extra_refs = refs[0], refs[1 : 1 + parts], refs[1 + parts : 1 + parts + extras]
    _, out_ref, factor_ref, acc = refs[1 + parts + extras :]
    sums = sum_refs[0][0:1, :]
    for s in sum_refs[1:]:
        sums = sums + s[0:1, :]
    token_scale = 1.0 / sums
    acc[...] = jnp.zeros_like(acc)

    def step(at):
        code = code_ref[at, :]
        factor = 1.0 / (total * jnp.sum(code * token_scale, axis=1, keepdims=True))
        factor_ref[at, :] = factor
        acc[...] += sublane_sums(code * factor)

    steps("middle", code_ref.shape[0], step)
    out_ref[0:1, :] = jnp.sum(acc[...], axis=0, keepdims=True)
    if extras:
        extra = extra_refs[0][...]
        for e in extra_refs[1:]:
            extra = extra + e[...]
        out_ref[1:2, :] = extra


def token_part(*refs, parts, scale, total, own):
    code_ref, centre_ref, tok_ref, factor_ref = refs[:4]
    sum_refs = refs[4 : 4 + parts]
    _, mine_ref, other_ref, scales_ref, acc = refs[4 + parts :]
    core = lax.rem(lax.axis_index("proto"), 2)
    sums = sum_refs[0][...]
    for s in sum_refs[1:]:
        sums = sums + s[...]
    scales_ref[...] = total / sums
    acc[...] = jnp.zeros_like(acc)
    token_scale, weight = scales_ref[0:1, :own], scales_ref[1:2, :own]

    def step(at):
        centre = centre_ref[at, :]
        pred = jnp.exp2(similarity(centre, tok_ref[:own, :]) * scale)
        logit = (pred * weight - code_ref[at, :own] * factor_ref[at, :] * token_scale).astype(BF16)
        acc[...] += lax.dot_general(
            centre, logit, (((0,), (0,)), ((), ())), preferred_element_type=F32
        )

    steps("token", code_ref.shape[0], step)
    acc[...] = acc[...] * total ** (-0.5)
    half = own // 2
    for c in range(2):

        @pl.when(core == c)
        def _():
            mine_ref[...] = acc[:, c * half : (c + 1) * half].T
            other_ref[...] = acc[:, (1 - c) * half : (2 - c) * half].T


def proto_part(code_ref, centre_ref, tok_ref, factor_ref, scales_ref, out_ref, *, scale):
    tokens = code_ref.shape[1]
    token_scale, weight = scales_ref[0:1, :], scales_ref[1:2, :]

    def step(at):
        pred = jnp.exp2(similarity(centre_ref[at, :], tok_ref[...]) * scale)
        logit = (pred * weight - code_ref[at, :] * factor_ref[at, :] * token_scale).astype(BF16)
        grad = jnp.dot(logit, tok_ref[...], preferred_element_type=F32)
        out_ref[at, :] = grad * tokens ** (-0.5)

    steps("proto", code_ref.shape[0], step)


def shifted(x, axis):
    n = lax.axis_size(axis)
    return [lax.ppermute(x, axis, [(i, (i + s) % n) for i in range(n)]) for s in range(1, n)]


def swapped(x, axis, mask):
    return lax.ppermute(x, axis, [(i, i ^ mask) for i in range(lax.axis_size(axis))])


def proto_terms(x):
    n = lax.axis_size("proto")
    x = x + swapped(x, "proto", 1)
    terms, unit = [x], 2
    while unit < n:
        group = min(4, n // unit)
        if unit > 2:
            terms = [sum(terms)]
        terms = [terms[0]] + [swapped(terms[0], "proto", unit * m) for m in range(1, group)]
        unit *= group
    return terms


def chip_sum(x):
    n, unit = lax.axis_size("proto"), 2
    while unit < n:
        group = min(4, n // unit)
        x = sum([swapped(x, "proto", unit * m) for m in range(1, group)], x)
        unit *= group
    return x


def local(first_view, alternate_augmentation, prototypes):
    own, d = first_view.shape
    k = prototypes.shape[0]
    tokens = own * lax.axis_size("dp")
    total = float(k * lax.axis_size("proto"))
    log2e = math.log2(math.e)
    code_scale = log2e / d / CODE_TEMP
    pred_scale = log2e / d / PRED_TEMP
    acc = pltpu.VMEM((8, tokens), F32)

    views = shifted(first_view, "dp")
    code, centres, columns = run(
        functools.partial(own_codes, scale=code_scale),
        [shape(k, tokens), shape(k, d, dtype=BF16), shape(k, 1)],
        [prototypes, first_view],
        [],
        keep=(0, 1, 2),
        us=3,
    )
    alternate_augmentation, columns = lax.optimization_barrier((alternate_augmentation, columns))
    others = shifted(alternate_augmentation, "dp")
    code, sums = run(
        functools.partial(first_pass, parts=len(views), scale=code_scale, total=total),
        [shape(1, tokens)],
        [code, centres, columns] + views,
        [pltpu.VMEM((tokens - own, d), BF16), acc],
        resident=list(range(1, 3 + len(views))),
        keep=[0],
        thread=True,
        us=7,
    )
    terms = proto_terms(sums)
    code, tok = run(
        target_rows,
        [shape(tokens, d, dtype=BF16)],
        [code, alternate_augmentation] + others,
        [],
        keep=[0],
        thread=True,
        us=1,
    )
    dens = []
    for i in range(2):
        code, den = run(
            functools.partial(
                denominators, scale=pred_scale, first=i * k // 2, last=(i + 1) * k // 2
            ),
            [shape(1, tokens)],
            [code, centres, tok],
            [acc],
            resident=[1, 2],
            keep=[0],
            thread=True,
            us=3,
        )
        dens.append(den)
        code, sums, factor = run(
            functools.partial(
                middle_pass, parts=len(terms), extras=2 * i, total=total
            ),
            [shape(1 + i, tokens), shape(k, 1)],
            [code] + terms + (dens if i else []),
            [acc],
            resident=list(range(1, 1 + len(terms) + 2 * i)),
            keep=[0, 1],
            thread=True,
            us=5,
        )
        terms = proto_terms(sums)
    code, mine, other, scales = run(
        functools.partial(token_part, parts=len(terms), scale=pred_scale, total=total, own=own),
        [shape(own // 2, d), shape(own // 2, d), shape(2, tokens)],
        [code, centres, tok, factor] + terms,
        [pltpu.VMEM((d, own), F32)],
        resident=list(range(1, 4 + len(terms))),
        keep=[0, 1, 2],
        thread=True,
        us=4,
    )
    mine = chip_sum(mine + swapped(other, "proto", 1))
    (proto_grad,) = run(
        functools.partial(proto_part, scale=pred_scale),
        [shape(k, d)],
        [code, centres, tok, factor, scales],
        [],
        resident=range(5),
        us=10,
    )
    mine, proto_grad = lax.optimization_barrier((mine, proto_grad))
    other = swapped(mine, "proto", 1)
    first = lax.rem(lax.axis_index("proto"), 2) == 0
    token_grad = jnp.where(
        first, jnp.concatenate([mine, other]), jnp.concatenate([other, mine])
    )
    return proto_grad, token_grad


def solution(mesh):
    return jax.shard_map(
        local,
        mesh=mesh,
        in_specs=(P("dp", None), P("dp", None), P("proto", None)),
        out_specs=(P("proto", None), P("dp", None)),
        check_vma=False,
    )
```

```python
import functools
import math

import jax
import jax.numpy as jnp
from jax import lax
from jax.experimental import pallas as pl
from jax.experimental.pallas import tpu as pltpu
from jax.sharding import PartitionSpec as P

CODE_TEMP = 0.05
PRED_TEMP = 0.1
F32 = jnp.float32
BF16 = jnp.bfloat16
VMEM_LIMIT = 20 << 20
CHUNK = 256
BLOCKS = {"own": 1024, "first": 1024, "den": 512, "middle": 512, "token": 2048, "proto": 1024}


def vmem_spec():
    return pl.BlockSpec(memory_space=pltpu.VMEM)


def shape(*dims, dtype=F32):
    return jax.ShapeDtypeStruct(dims, dtype)


def run(body, outs, args, scratch, resident=(), keep=(), us=1.0, thread=False):
    if thread:
        outs = [shape(*args[0].shape, dtype=args[0].dtype)] + outs
        keep = [0] + [i + 1 for i in keep]
        resident = [0] + list(resident)
    return pl.pallas_call(
        body,
        out_shape=tuple(pltpu.VMEM(s.shape, s.dtype) if i in keep else s for i, s in enumerate(outs)),
        in_specs=[vmem_spec()] * len(args),
        out_specs=tuple(vmem_spec() for _ in outs),
        scratch_shapes=scratch,
        input_output_aliases={0: 0} if thread else {},
        compiler_params=pltpu.CompilerParams(vmem_limit_bytes=VMEM_LIMIT),
        cost_estimate=pl.CostEstimate(flops=int(us * 1e9), bytes_accessed=1 << 20, transcendentals=0),
    )(
        *[
            pltpu.with_memory_space_constraint(a, pltpu.VMEM) if i in resident else a
            for i, a in enumerate(args)
        ]
    )


def normalize(values):
    floats = values.astype(F32)
    mean_square = jnp.mean(floats * floats, axis=-1, keepdims=True)
    return (floats * lax.rsqrt(mean_square + 1e-06)).astype(BF16)


def steps(name, size, step):
    block = min(BLOCKS[name], size)

    def body(i, carry):
        step(pl.ds(pl.multiple_of(i * block, block), block))
        return carry

    lax.fori_loop(0, size // block, body, 0)


def block_of(name, size):
    return min(BLOCKS[name], size // 2)


def pipelined(name, size, fill, work):
    block = block_of(name, size)
    n = size // block

    def at(i):
        return pl.ds(i * block if isinstance(i, int) else pl.multiple_of(i * block, block), block)

    def pair(i):
        fill(at(i), 1)
        work(at(i - 1), 0)
        fill(at(i + 1), 0)
        work(at(i), 1)

    def body(i, carry):
        pair(2 * i + 1)
        return carry

    fill(at(0), 0)
    lax.fori_loop(0, n // 2 - 1, body, 0)
    fill(at(n - 1), 1)
    work(at(n - 2), 0)
    work(at(n - 1), 1)


def chunks(first, last):
    width = min(CHUNK, last - first)
    return [slice(i, i + width) for i in range(first, last, width)]


def similarity(a, b):
    return lax.dot_general(a, b, (((1,), (1,)), ((), ())), preferred_element_type=F32)


def sublane_sums(block):
    return jnp.sum(block.reshape(block.shape[0] // 8, 8, block.shape[1]), axis=0)


def own_codes(proto_ref, token_ref, code_ref, centre_ref, column_ref, *, scale):
    own = token_ref.shape[0]
    tok = normalize(token_ref[...])

    def fill(at, slot):
        centre = normalize(proto_ref[at, :])
        centre_ref[at, :] = centre
        code_ref[at, :own] = jnp.exp2(similarity(centre, tok) * scale)

    def work(at, slot):
        column_ref[at, :] = jnp.sum(code_ref[at, :own], axis=1, keepdims=True)

    pipelined("own", proto_ref.shape[0], fill, work)


def first_pass(*refs, parts, scale, total):
    (_, centre_ref, column_ref), token_refs = refs[:3], refs[3 : 3 + parts]
    code_ref, out_ref, tok, acc = refs[3 + parts :]
    n = token_refs[0].shape[0]
    for i, t in enumerate(token_refs):
        tok[i * n : (i + 1) * n, :] = normalize(t[...])
    acc[...] = jnp.zeros_like(acc)

    def fill(at, slot):
        code_ref[at, n:] = jnp.exp2(similarity(centre_ref[at, :], tok[...]) * scale)

    def work(at, slot):
        columns = column_ref[at, :] + jnp.sum(code_ref[at, n:], axis=1, keepdims=True)
        factor = 1.0 / (total * columns)
        acc[...] += sublane_sums(code_ref[at, :] * factor)

    pipelined("first", centre_ref.shape[0], fill, work)
    out_ref[...] = jnp.sum(acc[...], axis=0, keepdims=True)


def denominators(_, centre_ref, tok_ref, code_ref, out_ref, acc, *slots, scale, first, size):
    acc[...] = jnp.zeros_like(acc)

    def fill(at, slot):
        centre = centre_ref[pl.ds(first + at.start, at.size), :]
        slots[slot][...] = similarity(centre, tok_ref[...])

    def work(at, slot):
        acc[...] += sublane_sums(jnp.exp2(slots[slot][...] * scale))

    pipelined("den", size, fill, work)
    out_ref[...] = jnp.sum(acc[...], axis=0, keepdims=True)


def target_rows(code_in, *refs):
    *token_refs, code_ref, tok = refs
    n = token_refs[0].shape[0]
    for i, t in enumerate(token_refs):
        tok[i * n : (i + 1) * n, :] = normalize(t[...])


def middle_pass(*refs, parts, extras, total):
    sum_refs, extra_refs = refs[1 : 1 + parts], refs[1 + parts : 1 + parts + extras]
    code_ref, out_ref, acc = refs[1 + parts + extras :]
    sums = sum_refs[0][0:1, :]
    for s in sum_refs[1:]:
        sums = sums + s[0:1, :]
    token_scale = 1.0 / sums
    acc[...] = jnp.zeros_like(acc)

    def step(at):
        code = code_ref[at, :]
        factor = 1.0 / (total * jnp.sum(code * token_scale, axis=1, keepdims=True))
        scaled = code * factor
        if extras:
            code_ref[at, :] = scaled
        acc[...] += sublane_sums(scaled)

    steps("middle", code_ref.shape[0], step)
    out_ref[0:1, :] = jnp.sum(acc[...], axis=0, keepdims=True)
    if extras:
        extra = extra_refs[0][...]
        for e in extra_refs[1:]:
            extra = extra + e[...]
        out_ref[1:2, :] = extra


def logit_block(centre, tok_ref, code_ref, scales_ref, logits, at, columns, scale):
    for c in columns:
        pred = jnp.exp2(similarity(centre, tok_ref[c, :]) * scale) * scales_ref[1:2, c]
        logits[:, c] = (pred - code_ref[at, c] * scales_ref[0:1, c]).astype(BF16)


def token_part(*refs, parts, scale, total, own):
    centre_ref, tok_ref = refs[1:3]
    sum_refs = refs[3 : 3 + parts]
    code_ref, mine_ref, other_ref, scales_ref, acc, *logits = refs[3 + parts :]
    core = lax.rem(lax.axis_index("proto"), 2)
    sums = sum_refs[0][...]
    for s in sum_refs[1:]:
        sums = sums + s[...]
    scales_ref[...] = total / sums
    acc[...] = jnp.zeros_like(acc)

    def fill(at, slot):
        logit_block(
            centre_ref[at, :], tok_ref, code_ref, scales_ref, logits[slot], at, chunks(0, own), scale
        )

    def work(at, slot):
        acc[...] += lax.dot_general(
            centre_ref[at, :], logits[slot][...], (((0,), (0,)), ((), ())), preferred_element_type=F32
        )

    pipelined("token", code_ref.shape[0], fill, work)
    acc[...] = acc[...] * total ** (-0.5)
    half = own // 2
    for c in range(2):

        @pl.when(core == c)
        def _():
            mine_ref[...] = acc[:, c * half : (c + 1) * half].T
            other_ref[...] = acc[:, (1 - c) * half : (2 - c) * half].T


def proto_part(code_ref, centre_ref, tok_ref, scales_ref, out_ref, *logits, scale):
    tokens = code_ref.shape[1]

    def fill(at, slot):
        logit_block(
            centre_ref[at, :], tok_ref, code_ref, scales_ref, logits[slot], at, chunks(0, tokens), scale
        )

    def work(at, slot):
        grad = jnp.dot(logits[slot][...], tok_ref[...], preferred_element_type=F32)
        out_ref[at, :] = grad * tokens ** (-0.5)

    pipelined("proto", code_ref.shape[0], fill, work)


def swapped(x, axis, mask):
    return lax.ppermute(x, axis, [(i, i ^ mask) for i in range(lax.axis_size(axis))])


def others_of(x, axis):
    return [swapped(x, axis, m) for m in range(lax.axis_size(axis) - 1, 0, -1)]


def proto_terms(x):
    n = lax.axis_size("proto")
    x = x + swapped(x, "proto", 1)
    terms, unit = [x], 2
    while unit < n:
        group = min(4, n // unit)
        if unit > 2:
            terms = [sum(terms)]
        terms = [terms[0]] + [swapped(terms[0], "proto", unit * m) for m in range(group - 1, 0, -1)]
        unit *= group
    return terms


def chip_sum(x):
    n, unit = lax.axis_size("proto"), 2
    while unit < n:
        group = min(4, n // unit)
        x = sum([swapped(x, "proto", unit * m) for m in range(group - 1, 0, -1)], x)
        unit *= group
    return x


def local(first_view, alternate_augmentation, prototypes):
    own, d = first_view.shape
    k = prototypes.shape[0]
    tokens = own * lax.axis_size("dp")
    total = float(k * lax.axis_size("proto"))
    log2e = math.log2(math.e)
    code_scale = log2e / d / CODE_TEMP
    pred_scale = log2e / d / PRED_TEMP
    acc = pltpu.VMEM((8, tokens), F32)

    def slots(name, size, columns, dtype=F32):
        return [pltpu.VMEM((block_of(name, size), columns), dtype)] * 2


    views = others_of(first_view, "dp")
    code, centres, columns = run(
        functools.partial(own_codes, scale=code_scale),
        [shape(k, tokens), shape(k, d, dtype=BF16), shape(k, 1)],
        [prototypes, first_view],
        [],
        keep=(0, 1, 2),
        us=3,
    )
    alternate_augmentation, columns = lax.optimization_barrier((alternate_augmentation, columns))
    others = others_of(alternate_augmentation, "dp")
    code, sums = run(
        functools.partial(first_pass, parts=len(views), scale=code_scale, total=total),
        [shape(1, tokens)],
        [code, centres, columns] + views,
        [pltpu.VMEM((tokens - own, d), BF16), acc],
        resident=list(range(1, 3 + len(views))),
        keep=[0],
        thread=True,
        us=7,
    )
    terms = proto_terms(sums)
    code, tok = run(
        target_rows,
        [shape(tokens, d, dtype=BF16)],
        [code, alternate_augmentation] + others,
        [],
        keep=[0],
        thread=True,
        us=1,
    )
    dens = []
    for i in range(2):
        code, den = run(
            functools.partial(denominators, scale=pred_scale, first=i * k // 2, size=k // 2),
            [shape(1, tokens)],
            [code, centres, tok],
            [acc] + slots("den", k // 2, tokens),
            resident=[1, 2],
            keep=[0],
            thread=True,
            us=3,
        )
        dens.append(den)
        code, sums = run(
            functools.partial(
                middle_pass, parts=len(terms), extras=2 * i, total=total
            ),
            [shape(1 + i, tokens)],
            [code] + terms + (dens if i else []),
            [acc],
            resident=list(range(1, 1 + len(terms) + 2 * i)),
            keep=[0],
            thread=True,
            us=5,
        )
        terms = proto_terms(sums)
    code, mine, other, scales = run(
        functools.partial(token_part, parts=len(terms), scale=pred_scale, total=total, own=own),
        [shape(own // 2, d), shape(own // 2, d), shape(2, tokens)],
        [code, centres, tok] + terms,
        [pltpu.VMEM((d, own), F32)] + slots("token", k, own, BF16),
        resident=list(range(1, 3 + len(terms))),
        keep=[0, 1, 2],
        thread=True,
        us=4,
    )
    mine = chip_sum(mine + swapped(other, "proto", 1))
    (proto_grad,) = run(
        functools.partial(proto_part, scale=pred_scale),
        [shape(k, d)],
        [code, centres, tok, scales],
        slots("proto", k, tokens, BF16),
        resident=range(4),
        us=10,
    )
    mine, proto_grad = lax.optimization_barrier((mine, proto_grad))
    other = swapped(mine, "proto", 1)
    first = lax.rem(lax.axis_index("proto"), 2) == 0
    token_grad = jnp.where(
        first, jnp.concatenate([mine, other]), jnp.concatenate([other, mine])
    )
    return proto_grad, token_grad


def solution(mesh):
    return jax.shard_map(
        local,
        mesh=mesh,
        in_specs=(P("dp", None), P("dp", None), P("proto", None)),
        out_specs=(P("proto", None), P("dp", None)),
        check_vma=False,
    )
```

```python
import functools
import math

import jax
import jax.numpy as jnp
from jax import lax
from jax.experimental import pallas as pl
from jax.experimental.pallas import tpu as pltpu
from jax.sharding import PartitionSpec as P

CODE_TEMP = 0.05
PRED_TEMP = 0.1
F32 = jnp.float32
BF16 = jnp.bfloat16
VMEM_LIMIT = 20 << 20
CHUNK = 256
BLOCKS = {"own": 2048, "first": 1024, "den": 2048, "middle": 512, "token": 2048}
SPLIT = 3
TILE = 16


def vmem_spec():
    return pl.BlockSpec(memory_space=pltpu.VMEM)


def shape(*dims, dtype=F32):
    return jax.ShapeDtypeStruct(dims, dtype)


def run(body, outs, args, scratch, resident=(), keep=(), us=1.0, thread=False):
    if thread:
        outs = [shape(*args[0].shape, dtype=args[0].dtype)] + outs
        keep = [0] + [i + 1 for i in keep]
        resident = [0] + list(resident)
    return pl.pallas_call(
        body,
        out_shape=tuple(pltpu.VMEM(s.shape, s.dtype) if i in keep else s for i, s in enumerate(outs)),
        in_specs=[vmem_spec()] * len(args),
        out_specs=tuple(vmem_spec() for _ in outs),
        scratch_shapes=scratch,
        input_output_aliases={0: 0} if thread else {},
        compiler_params=pltpu.CompilerParams(vmem_limit_bytes=VMEM_LIMIT),
        cost_estimate=pl.CostEstimate(flops=int(us * 1e9), bytes_accessed=1 << 20, transcendentals=0),
    )(
        *[
            pltpu.with_memory_space_constraint(a, pltpu.VMEM) if i in resident else a
            for i, a in enumerate(args)
        ]
    )


def normalize(values):
    floats = values.astype(F32)
    mean_square = jnp.mean(floats * floats, axis=-1, keepdims=True)
    return (floats * lax.rsqrt(mean_square + 1e-06)).astype(BF16)


def steps(name, size, step):
    block = min(BLOCKS[name], size)

    def body(i, carry):
        step(pl.ds(pl.multiple_of(i * block, block), block))
        return carry

    lax.fori_loop(0, size // block, body, 0)


def block_of(name, size):
    return min(BLOCKS[name], size // 2)


def pipelined(n, fill, work):
    def body(i, carry):
        fill(2 * i + 1, 1)
        work(2 * i, 0)
        fill(2 * i + 2, 0)
        work(2 * i + 1, 1)
        return carry

    fill(0, 0)
    lax.fori_loop(0, n // 2 - 1, body, 0)
    fill(n - 1, 1)
    work(n - 2, 0)
    work(n - 1, 1)


def part(i, size):
    return pl.ds(i * size if isinstance(i, int) else pl.multiple_of(i * size, size), size)


def similarity(a, b):
    return lax.dot_general(a, b, (((1,), (1,)), ((), ())), preferred_element_type=F32)


def sublane_sums(block):
    return jnp.sum(block.reshape(block.shape[0] // 8, 8, block.shape[1]), axis=0)


def lane_sums(block):
    return sum(block[:, i : i + 128] for i in range(0, block.shape[1], 128))


def own_codes(proto_ref, token_ref, code_ref, centre_ref, column_ref, *, scale):
    own = token_ref.shape[0]
    tok = normalize(token_ref[...])

    def step(at):
        centre = normalize(proto_ref[at, :])
        centre_ref[at, :] = centre
        code = jnp.exp2(similarity(centre, tok) * scale)
        code_ref[at, :own] = code
        column_ref[at, :] = lane_sums(code)

    steps("own", proto_ref.shape[0], step)


def first_pass(*refs, parts, scale, total):
    (_, centre_ref, column_ref), token_refs = refs[:3], refs[3 : 3 + parts]
    code_ref, out_ref, tok, acc, columns = refs[3 + parts :]
    n = token_refs[0].shape[0]
    for i, t in enumerate(token_refs):
        tok[i * n : (i + 1) * n, :] = normalize(t[...])
    acc[...] = jnp.zeros_like(acc)
    block = block_of("first", centre_ref.shape[0])

    def fill(i, slot):
        at = part(i, block)
        code = jnp.exp2(similarity(centre_ref[at, :], tok[...]) * scale)
        code_ref[at, n:] = code
        columns[at, :] = column_ref[at, :] + lane_sums(code)

    def work(i, slot):
        at = part(i, block)
        factor = 1.0 / (total * jnp.sum(columns[at, :], axis=1, keepdims=True))
        acc[...] += sublane_sums(code_ref[at, :] * factor)

    pipelined(centre_ref.shape[0] // block, fill, work)
    out_ref[...] = jnp.sum(acc[...], axis=0, keepdims=True)


def denominators(_, centre_ref, token_ref, code_ref, tok_ref, out_ref, acc, *, scale):
    tok_ref[...] = normalize(token_ref[...])
    acc[...] = jnp.zeros_like(acc)

    def step(at):
        acc[...] += sublane_sums(jnp.exp2(similarity(centre_ref[at, :], tok_ref[...]) * scale))

    steps("den", centre_ref.shape[0], step)
    out_ref[...] = jnp.sum(acc[...], axis=0, keepdims=True)


def term_sum(refs):
    return functools.reduce(lambda a, b: a + b, [r[...] for r in refs])


def middle_pass(*refs, parts, total):
    den_ref, (code_ref, out_ref, acc) = refs[1 + parts], refs[2 + parts :]
    token_scale = 1.0 / term_sum(refs[1 : 1 + parts])
    acc[...] = jnp.zeros_like(acc)

    def step(at):
        code = code_ref[at, :]
        factor = 1.0 / (total * jnp.sum(code * token_scale, axis=1, keepdims=True))
        acc[...] += sublane_sums(code * factor)

    steps("middle", code_ref.shape[0], step)
    tokens = acc.shape[1]
    out_ref[:, :tokens] = jnp.sum(acc[...], axis=0, keepdims=True)
    out_ref[:, tokens:] = den_ref[...]


def last_pass(*refs, parts, total):
    tok_ref, (code_ref, out_ref, weight_ref, pack_ref, acc) = refs[1 + parts], refs[2 + parts :]
    tokens, own = acc.shape[1], tok_ref.shape[0]
    sums = term_sum(refs[1 : 1 + parts])
    token_scale = 1.0 / sums[:, :tokens]
    weight = total / sums[:, tokens:]
    weight_ref[...] = weight
    pack_ref[:own, :] = tok_ref[...]
    lines = [weight[:, i : i + 128] for i in range(0, own, 128)]
    pieces, rest = [], jnp.concatenate(lines, axis=0)
    for _ in range(SPLIT):
        piece = rest.astype(BF16).astype(F32)
        pieces.append(piece)
        rest = rest - piece
    rows = SPLIT * len(lines)
    pad = -rows % TILE
    pack_ref[own:, :] = jnp.concatenate(pieces + [jnp.zeros((pad, 128), F32)], axis=0).astype(BF16)
    acc[...] = jnp.zeros_like(acc)

    def step(at):
        code = code_ref[at, :]
        factor = 1.0 / (total * jnp.sum(code * token_scale, axis=1, keepdims=True))
        scaled = code * factor
        code_ref[at, :] = scaled
        acc[...] += sublane_sums(scaled)

    steps("middle", code_ref.shape[0], step)
    out_ref[...] = jnp.sum(acc[...], axis=0, keepdims=True)


def logit(centre, tok, code, token_scale, weight, scale):
    pred = jnp.exp2(similarity(centre, tok) * scale) * weight
    return (pred - code * token_scale).astype(BF16)


def token_part(*refs, parts, scale, total):
    centre_ref, tok_ref, weight_ref = refs[1:4]
    code_ref, mine_ref, other_ref, scale_ref, logit_ref, acc = refs[4 + parts :]
    own = tok_ref.shape[0]
    core = lax.rem(lax.axis_index("proto"), 2)
    scale_ref[...] = total / term_sum(refs[4 : 4 + parts])
    acc[...] = jnp.zeros_like(acc)
    block = block_of("token", code_ref.shape[0])

    def fill(i, slot):
        at = part(i, block)
        for c in range(0, own, CHUNK):
            c = slice(c, min(c + CHUNK, own))
            logit_ref[at, c] = logit(
                centre_ref[at, :], tok_ref[c, :], code_ref[at, c], scale_ref[:, c], weight_ref[:, c], scale
            )

    def work(i, slot):
        at = part(i, block)
        acc[...] += lax.dot_general(
            centre_ref[at, :], logit_ref[at, :], (((0,), (0,)), ((), ())), preferred_element_type=F32
        )

    pipelined(code_ref.shape[0] // block, fill, work)
    acc[...] = acc[...] * total ** (-0.5)
    half = own // 2
    for c in range(2):

        @pl.when(core == c)
        def _():
            mine_ref[...] = acc[:, c * half : (c + 1) * half].T
            other_ref[...] = acc[:, (1 - c) * half : (2 - c) * half].T


def proto_part(*refs, parts, scale):
    (code_ref, centre_ref, tok_ref, scale_ref, logit_ref), packs = refs[:5], refs[5 : 5 + parts]
    out_ref, tok, weight, *slots = refs[5 + parts :]
    tokens, own = code_ref.shape[1], tok_ref.shape[0]
    for i, pack in enumerate(packs):
        tok[i * own : (i + 1) * own, :] = pack[:own, :]
        pieces = pack[own:, :].astype(F32)
        count = own // 128
        lines = sum(pieces[j * count : (j + 1) * count, :] for j in range(SPLIT))
        for j in range(count):
            at = i * own + j * 128
            weight[:, at : at + 128] = lines[j : j + 1, :]

    def fill(i, slot):
        at = part(i, CHUNK)
        c = pl.ds(pl.multiple_of(own + i * CHUNK, 128), CHUNK)
        slots[slot][...] = logit(
            centre_ref[...], tok[at, :], code_ref[:, c], scale_ref[:, c], weight[:, at], scale
        )

    def work(i, slot):
        out_ref[...] += jnp.dot(slots[slot][...], tok[part(i, CHUNK), :], preferred_element_type=F32)

    out_ref[...] = jnp.dot(logit_ref[...], tok_ref[...], preferred_element_type=F32)
    pipelined(parts * own // CHUNK, fill, work)
    out_ref[...] = out_ref[...] * tokens ** (-0.5)


def swapped(x, axis, mask):
    return lax.ppermute(x, axis, [(i, i ^ mask) for i in range(lax.axis_size(axis))])


def others_of(x, axis):
    return [swapped(x, axis, m) for m in range(lax.axis_size(axis) - 1, 0, -1)]


def proto_terms(x):
    n = lax.axis_size("proto")
    x = x + swapped(x, "proto", 1)
    terms, unit = [x], 2
    while unit < n:
        group = min(4, n // unit)
        if unit > 2:
            terms = [sum(terms)]
        terms = [terms[0]] + [swapped(terms[0], "proto", unit * m) for m in range(group - 1, 0, -1)]
        unit *= group
    return terms


def chip_sum(x):
    n, unit = lax.axis_size("proto"), 2
    while unit < n:
        group = min(4, n // unit)
        x = sum([swapped(x, "proto", unit * m) for m in range(group - 1, 0, -1)], x)
        unit *= group
    return x


def local(first_view, alternate_augmentation, prototypes):
    own, d = first_view.shape
    k = prototypes.shape[0]
    tokens = own * lax.axis_size("dp")
    total = float(k * lax.axis_size("proto"))
    log2e = math.log2(math.e)
    code_scale = log2e / d / CODE_TEMP
    pred_scale = log2e / d / PRED_TEMP
    acc = pltpu.VMEM((8, tokens), F32)

    views = others_of(first_view, "dp")
    code, centres, columns = run(
        functools.partial(own_codes, scale=code_scale),
        [shape(k, tokens), shape(k, d, dtype=BF16), shape(k, 128)],
        [prototypes, first_view],
        [],
        keep=(0, 1, 2),
        us=3,
    )
    parts = len(views)
    code, sums = run(
        functools.partial(first_pass, parts=parts, scale=code_scale, total=total),
        [shape(1, tokens)],
        [code, centres, columns] + views,
        [pltpu.VMEM((tokens - own, d), BF16), acc, pltpu.VMEM((k, 128), F32)],
        resident=list(range(1, 3 + parts)),
        keep=[0],
        thread=True,
        us=7,
    )
    terms = proto_terms(sums)
    code, tok, den = run(
        functools.partial(denominators, scale=pred_scale),
        [shape(own, d, dtype=BF16), shape(1, own)],
        [code, centres, alternate_augmentation],
        [pltpu.VMEM((8, own), F32)],
        resident=[1],
        keep=[0, 1],
        thread=True,
        us=2,
    )
    code, sums = run(
        functools.partial(middle_pass, parts=len(terms), total=total),
        [shape(1, tokens + own)],
        [code] + terms + [den],
        [acc],
        resident=list(range(1, 2 + len(terms))),
        keep=[0],
        thread=True,
        us=5,
    )
    terms = proto_terms(sums)
    pack_rows = own + -(-SPLIT * own // 128 // TILE) * TILE
    code, sums, weight, pack = run(
        functools.partial(last_pass, parts=len(terms), total=total),
        [shape(1, tokens), shape(1, own), shape(pack_rows, d, dtype=BF16)],
        [code] + terms + [tok],
        [acc],
        resident=list(range(1, 2 + len(terms))),
        keep=[0, 1, 2],
        thread=True,
        us=5,
    )
    terms = proto_terms(sums)
    packs = others_of(pack, "dp")
    code, mine, other, token_scale, logits = run(
        functools.partial(token_part, parts=len(terms), scale=pred_scale, total=total),
        [shape(own // 2, d), shape(own // 2, d), shape(1, tokens), shape(k, own, dtype=BF16)],
        [code, centres, tok, weight] + terms,
        [pltpu.VMEM((d, own), F32)],
        resident=list(range(1, 4 + len(terms))),
        keep=[0, 1, 2, 3],
        thread=True,
        us=4,
    )
    mine = chip_sum(mine + swapped(other, "proto", 1))
    (proto_grad,) = run(
        functools.partial(proto_part, parts=parts, scale=pred_scale),
        [shape(k, d)],
        [code, centres, tok, token_scale, logits] + packs,
        [pltpu.VMEM((tokens - own, d), BF16), pltpu.VMEM((1, tokens - own), F32)]
        + [pltpu.VMEM((k, CHUNK), BF16)] * 2,
        resident=range(5 + parts),
        us=10,
    )
    mine, proto_grad = lax.optimization_barrier((mine, proto_grad))
    other = swapped(mine, "proto", 1)
    first = lax.rem(lax.axis_index("proto"), 2) == 0
    token_grad = jnp.where(
        first, jnp.concatenate([mine, other]), jnp.concatenate([other, mine])
    )
    return proto_grad, token_grad


def solution(mesh):
    return jax.shard_map(
        local,
        mesh=mesh,
        in_specs=(P("dp", None), P("dp", None), P("proto", None)),
        out_specs=(P("proto", None), P("dp", None)),
        check_vma=False,
    )
```

```python
import functools
import math

import jax
import jax.numpy as jnp
from jax import lax
from jax.experimental import pallas as pl
from jax.experimental.pallas import tpu as pltpu
from jax.sharding import PartitionSpec as P

CODE_TEMP = 0.05
PRED_TEMP = 0.1
F32 = jnp.float32
BF16 = jnp.bfloat16
VMEM_LIMIT = 20 << 20
CHUNK = 256
BLOCKS = {"own": 2048, "first": 1024, "den": 2048, "middle": 512, "token": 2048}
SUBS = {"first": 1, "proto": 1}
SPLIT = 3
TILE = 16


def vmem_spec():
    return pl.BlockSpec(memory_space=pltpu.VMEM)


def shape(*dims, dtype=F32):
    return jax.ShapeDtypeStruct(dims, dtype)


def run(body, outs, args, scratch, resident=(), keep=(), us=1.0, thread=False):
    if thread:
        outs = [shape(*args[0].shape, dtype=args[0].dtype)] + outs
        keep = [0] + [i + 1 for i in keep]
        resident = [0] + list(resident)
    return pl.pallas_call(
        body,
        out_shape=tuple(pltpu.VMEM(s.shape, s.dtype) if i in keep else s for i, s in enumerate(outs)),
        in_specs=[vmem_spec()] * len(args),
        out_specs=tuple(vmem_spec() for _ in outs),
        scratch_shapes=scratch,
        input_output_aliases={0: 0} if thread else {},
        compiler_params=pltpu.CompilerParams(vmem_limit_bytes=VMEM_LIMIT),
        cost_estimate=pl.CostEstimate(flops=int(us * 1e9), bytes_accessed=1 << 20, transcendentals=0),
    )(
        *[
            pltpu.with_memory_space_constraint(a, pltpu.VMEM) if i in resident else a
            for i, a in enumerate(args)
        ]
    )


def normalize(values):
    floats = values.astype(F32)
    mean_square = jnp.mean(floats * floats, axis=-1, keepdims=True)
    return (floats * lax.rsqrt(mean_square + 1e-06)).astype(BF16)


def steps(name, size, step):
    block = min(BLOCKS[name], size)

    def body(i, carry):
        step(pl.ds(pl.multiple_of(i * block, block), block))
        return carry

    lax.fori_loop(0, size // block, body, 0)


def block_of(name, size):
    return min(BLOCKS[name], size // 2)


def pipelined(n, fill, work, subs=1):
    def both(i, slot):
        for m in range(subs):
            fill(i, slot, m)
            work(i - 1, 1 - slot, m)

    def body(i, carry):
        both(2 * i + 1, 1)
        both(2 * i + 2, 0)
        return carry

    for m in range(subs):
        fill(0, 0, m)
    if n <= 4:
        for i in range(1, n - 1):
            both(i, i % 2)
    else:
        lax.fori_loop(0, n // 2 - 1, body, 0)
    both(n - 1, 1)
    for m in range(subs):
        work(n - 1, 1, m)


def part(i, size):
    return pl.ds(i * size if isinstance(i, int) else pl.multiple_of(i * size, size), size)


def similarity(a, b):
    return lax.dot_general(a, b, (((1,), (1,)), ((), ())), preferred_element_type=F32)


def sublane_sums(block):
    return jnp.sum(block.reshape(block.shape[0] // 8, 8, block.shape[1]), axis=0)


def lane_sums(block):
    return sum(block[:, i : i + 128] for i in range(0, block.shape[1], 128))


def own_codes(proto_ref, token_ref, code_ref, centre_ref, column_ref, *, scale):
    own = token_ref.shape[0]
    tok = normalize(token_ref[...])

    def step(at):
        centre = normalize(proto_ref[at, :])
        centre_ref[at, :] = centre
        code = jnp.exp2(similarity(centre, tok) * scale)
        code_ref[at, :own] = code
        column_ref[at, :] = lane_sums(code)

    steps("own", proto_ref.shape[0], step)


def first_pass(*refs, parts, scale, total):
    (_, centre_ref, column_ref), token_refs = refs[:3], refs[3 : 3 + parts]
    code_ref, out_ref, tok, acc, columns = refs[3 + parts :]
    n = token_refs[0].shape[0]
    for i, t in enumerate(token_refs):
        tok[i * n : (i + 1) * n, :] = normalize(t[...])
    acc[...] = jnp.zeros_like(acc)
    block = block_of("first", centre_ref.shape[0])

    size = block // SUBS["first"]

    def rows(i, m):
        start = i * block + m * size
        return pl.ds(start if isinstance(i, int) else pl.multiple_of(start, size), size)

    def fill(i, slot, m):
        at = rows(i, m)
        code = jnp.exp2(similarity(centre_ref[at, :], tok[...]) * scale)
        code_ref[at, n:] = code
        columns[at, :] = column_ref[at, :] + lane_sums(code)

    def work(i, slot, m):
        at = rows(i, m)
        factor = 1.0 / (total * jnp.sum(columns[at, :], axis=1, keepdims=True))
        acc[...] += sublane_sums(code_ref[at, :] * factor)

    pipelined(centre_ref.shape[0] // block, fill, work, SUBS["first"])
    out_ref[...] = jnp.sum(acc[...], axis=0, keepdims=True)


def denominators(_, centre_ref, token_ref, code_ref, tok_ref, out_ref, acc, *, scale):
    tok_ref[...] = normalize(token_ref[...])
    acc[...] = jnp.zeros_like(acc)

    def step(at):
        acc[...] += sublane_sums(jnp.exp2(similarity(centre_ref[at, :], tok_ref[...]) * scale))

    steps("den", centre_ref.shape[0], step)
    out_ref[...] = jnp.sum(acc[...], axis=0, keepdims=True)


def term_sum(refs):
    return functools.reduce(lambda a, b: a + b, [r[...] for r in refs])


def middle_pass(*refs, parts, total):
    den_ref, (code_ref, out_ref, acc) = refs[1 + parts], refs[2 + parts :]
    token_scale = 1.0 / term_sum(refs[1 : 1 + parts])
    acc[...] = jnp.zeros_like(acc)

    def step(at):
        code = code_ref[at, :]
        factor = 1.0 / (total * jnp.sum(code * token_scale, axis=1, keepdims=True))
        acc[...] += sublane_sums(code * factor)

    steps("middle", code_ref.shape[0], step)
    tokens = acc.shape[1]
    out_ref[:, :tokens] = jnp.sum(acc[...], axis=0, keepdims=True)
    out_ref[:, tokens:] = den_ref[...]


def last_pass(*refs, parts, total):
    tok_ref, (code_ref, out_ref, weight_ref, pack_ref, acc) = refs[1 + parts], refs[2 + parts :]
    tokens, own = acc.shape[1], tok_ref.shape[0]
    sums = term_sum(refs[1 : 1 + parts])
    token_scale = 1.0 / sums[:, :tokens]
    weight = total / sums[:, tokens:]
    weight_ref[...] = weight
    pack_ref[:own, :] = tok_ref[...]
    lines = [weight[:, i : i + 128] for i in range(0, own, 128)]
    pieces, rest = [], jnp.concatenate(lines, axis=0)
    for _ in range(SPLIT):
        piece = rest.astype(BF16).astype(F32)
        pieces.append(piece)
        rest = rest - piece
    rows = SPLIT * len(lines)
    pad = -rows % TILE
    pack_ref[own:, :] = jnp.concatenate(pieces + [jnp.zeros((pad, 128), F32)], axis=0).astype(BF16)
    acc[...] = jnp.zeros_like(acc)

    def step(at):
        code = code_ref[at, :]
        factor = 1.0 / (total * jnp.sum(code * token_scale, axis=1, keepdims=True))
        scaled = code * factor
        code_ref[at, :] = scaled
        acc[...] += sublane_sums(scaled)

    steps("middle", code_ref.shape[0], step)
    out_ref[...] = jnp.sum(acc[...], axis=0, keepdims=True)


def logit(centre, tok, code, token_scale, weight, scale):
    pred = jnp.exp2(similarity(centre, tok) * scale) * weight
    return (pred - code * token_scale).astype(BF16)


def token_part(*refs, parts, scale, total):
    centre_ref, tok_ref, weight_ref = refs[1:4]
    code_ref, mine_ref, other_ref, scale_ref, logit_ref, acc = refs[4 + parts :]
    own = tok_ref.shape[0]
    core = lax.rem(lax.axis_index("proto"), 2)
    scale_ref[...] = total / term_sum(refs[4 : 4 + parts])
    acc[...] = jnp.zeros_like(acc)
    block = block_of("token", code_ref.shape[0])

    def fill(i, slot, m):
        at = part(i, block)
        for c in range(0, own, CHUNK):
            c = slice(c, min(c + CHUNK, own))
            logit_ref[at, c] = logit(
                centre_ref[at, :], tok_ref[c, :], code_ref[at, c], scale_ref[:, c], weight_ref[:, c], scale
            )

    def work(i, slot, m):
        at = part(i, block)
        acc[...] += lax.dot_general(
            centre_ref[at, :], logit_ref[at, :], (((0,), (0,)), ((), ())), preferred_element_type=F32
        )

    pipelined(code_ref.shape[0] // block, fill, work)
    acc[...] = acc[...] * total ** (-0.5)
    half = own // 2
    for c in range(2):

        @pl.when(core == c)
        def _():
            mine_ref[...] = acc[:, c * half : (c + 1) * half].T
            other_ref[...] = acc[:, (1 - c) * half : (2 - c) * half].T


def proto_part(*refs, parts, scale):
    (code_ref, centre_ref, tok_ref, scale_ref, logit_ref), packs = refs[:5], refs[5 : 5 + parts]
    out_ref, tok, weight, *slots = refs[5 + parts :]
    tokens, own = code_ref.shape[1], tok_ref.shape[0]
    for i, pack in enumerate(packs):
        tok[i * own : (i + 1) * own, :] = pack[:own, :]
        pieces = pack[own:, :].astype(F32)
        count = own // 128
        lines = sum(pieces[j * count : (j + 1) * count, :] for j in range(SPLIT))
        for j in range(count):
            at = i * own + j * 128
            weight[:, at : at + 128] = lines[j : j + 1, :]

    subs = SUBS["proto"]
    size = code_ref.shape[0] // subs

    def fill(i, slot, m):
        at = part(i, CHUNK)
        c = pl.ds(pl.multiple_of(own + i * CHUNK, 128), CHUNK)
        r = slice(m * size, (m + 1) * size)
        slots[slot][r, :] = logit(
            centre_ref[r, :], tok[at, :], code_ref[r, c], scale_ref[:, c], weight[:, at], scale
        )

    def work(i, slot, m):
        r = slice(m * size, (m + 1) * size)
        out_ref[r, :] += jnp.dot(slots[slot][r, :], tok[part(i, CHUNK), :], preferred_element_type=F32)

    out_ref[...] = jnp.dot(logit_ref[...], tok_ref[...], preferred_element_type=F32)
    pipelined(parts * own // CHUNK, fill, work, subs)
    out_ref[...] = out_ref[...] * tokens ** (-0.5)


def swapped(x, axis, mask):
    return lax.ppermute(x, axis, [(i, i ^ mask) for i in range(lax.axis_size(axis))])


def others_of(x, axis):
    return [swapped(x, axis, m) for m in range(lax.axis_size(axis) - 1, 0, -1)]


def proto_terms(x):
    n = lax.axis_size("proto")
    x = x + swapped(x, "proto", 1)
    terms, unit = [x], 2
    while unit < n:
        group = min(4, n // unit)
        if unit > 2:
            terms = [sum(terms)]
        terms = [terms[0]] + [swapped(terms[0], "proto", unit * m) for m in range(group - 1, 0, -1)]
        unit *= group
    return terms


def chip_sum(x):
    n, unit = lax.axis_size("proto"), 2
    while unit < n:
        group = min(4, n // unit)
        x = sum([swapped(x, "proto", unit * m) for m in range(group - 1, 0, -1)], x)
        unit *= group
    return x


def local(first_view, alternate_augmentation, prototypes):
    own, d = first_view.shape
    k = prototypes.shape[0]
    tokens = own * lax.axis_size("dp")
    total = float(k * lax.axis_size("proto"))
    log2e = math.log2(math.e)
    code_scale = log2e / d / CODE_TEMP
    pred_scale = log2e / d / PRED_TEMP
    acc = pltpu.VMEM((8, tokens), F32)

    views = others_of(first_view, "dp")
    code, centres, columns = run(
        functools.partial(own_codes, scale=code_scale),
        [shape(k, tokens), shape(k, d, dtype=BF16), shape(k, 128)],
        [prototypes, first_view],
        [],
        keep=(0, 1, 2),
        us=3,
    )
    parts = len(views)
    code, sums = run(
        functools.partial(first_pass, parts=parts, scale=code_scale, total=total),
        [shape(1, tokens)],
        [code, centres, columns] + views,
        [pltpu.VMEM((tokens - own, d), BF16), acc, pltpu.VMEM((k, 128), F32)],
        resident=list(range(1, 3 + parts)),
        keep=[0],
        thread=True,
        us=7,
    )
    terms = proto_terms(sums)
    code, tok, den = run(
        functools.partial(denominators, scale=pred_scale),
        [shape(own, d, dtype=BF16), shape(1, own)],
        [code, centres, alternate_augmentation],
        [pltpu.VMEM((8, own), F32)],
        resident=[1],
        keep=[0, 1],
        thread=True,
        us=2,
    )
    code, sums = run(
        functools.partial(middle_pass, parts=len(terms), total=total),
        [shape(1, tokens + own)],
        [code] + terms + [den],
        [acc],
        resident=list(range(1, 2 + len(terms))),
        keep=[0],
        thread=True,
        us=5,
    )
    terms = proto_terms(sums)
    terms = terms[:1] + terms[2:] + terms[1:2]
    pack_rows = own + -(-SPLIT * own // 128 // TILE) * TILE
    code, sums, weight, pack = run(
        functools.partial(last_pass, parts=len(terms), total=total),
        [shape(1, tokens), shape(1, own), shape(pack_rows, d, dtype=BF16)],
        [code] + terms + [tok],
        [acc],
        resident=list(range(1, 2 + len(terms))),
        keep=[0, 1, 2],
        thread=True,
        us=5,
    )
    terms = proto_terms(sums)
    packs = others_of(pack, "dp")
    code, mine, other, token_scale, logits = run(
        functools.partial(token_part, parts=len(terms), scale=pred_scale, total=total),
        [shape(own // 2, d), shape(own // 2, d), shape(1, tokens), shape(k, own, dtype=BF16)],
        [code, centres, tok, weight] + terms,
        [pltpu.VMEM((d, own), F32)],
        resident=list(range(1, 4 + len(terms))),
        keep=[0, 1, 2, 3],
        thread=True,
        us=4,
    )
    mine = chip_sum(mine + swapped(other, "proto", 1))
    (proto_grad,) = run(
        functools.partial(proto_part, parts=parts, scale=pred_scale),
        [shape(k, d)],
        [code, centres, tok, token_scale, logits] + packs,
        [pltpu.VMEM((tokens - own, d), BF16), pltpu.VMEM((1, tokens - own), F32)]
        + [pltpu.VMEM((k, CHUNK), BF16)] * 2,
        resident=range(5 + parts),
        us=10,
    )
    mine, proto_grad = lax.optimization_barrier((mine, proto_grad))
    other = swapped(mine, "proto", 1)
    first = lax.rem(lax.axis_index("proto"), 2) == 0
    token_grad = jnp.where(
        first, jnp.concatenate([mine, other]), jnp.concatenate([other, mine])
    )
    return proto_grad, token_grad


def solution(mesh):
    return jax.shard_map(
        local,
        mesh=mesh,
        in_specs=(P("dp", None), P("dp", None), P("proto", None)),
        out_specs=(P("proto", None), P("dp", None)),
        check_vma=False,
    )
```

```python
import functools
import math

import jax
import jax.numpy as jnp
from jax import lax
from jax.experimental import pallas as pl
from jax.experimental.pallas import tpu as pltpu
from jax.sharding import PartitionSpec as P

CODE_TEMP = 0.05
PRED_TEMP = 0.1
F32 = jnp.float32
BF16 = jnp.bfloat16
VMEM_LIMIT = 20 << 20
CHUNK = 256
BLOCKS = {"own": 2048, "first": 1024, "den": 2048, "middle": 512, "token": 2048}
SUBS = {"first": 1, "proto": 1}
SPLIT = 3
TILE = 16


def vmem_spec():
    return pl.BlockSpec(memory_space=pltpu.VMEM)


def shape(*dims, dtype=F32):
    return jax.ShapeDtypeStruct(dims, dtype)


def run(body, outs, args, scratch, resident=(), keep=(), us=1.0, thread=False):
    if thread:
        outs = [shape(*args[0].shape, dtype=args[0].dtype)] + outs
        keep = [0] + [i + 1 for i in keep]
        resident = [0] + list(resident)
    return pl.pallas_call(
        body,
        out_shape=tuple(pltpu.VMEM(s.shape, s.dtype) if i in keep else s for i, s in enumerate(outs)),
        in_specs=[vmem_spec()] * len(args),
        out_specs=tuple(vmem_spec() for _ in outs),
        scratch_shapes=scratch,
        input_output_aliases={0: 0} if thread else {},
        compiler_params=pltpu.CompilerParams(vmem_limit_bytes=VMEM_LIMIT),
        cost_estimate=pl.CostEstimate(flops=int(us * 1e9), bytes_accessed=1 << 20, transcendentals=0),
    )(
        *[
            pltpu.with_memory_space_constraint(a, pltpu.VMEM) if i in resident else a
            for i, a in enumerate(args)
        ]
    )


def normalize(values):
    floats = values.astype(F32)
    mean_square = jnp.mean(floats * floats, axis=-1, keepdims=True)
    return (floats * lax.rsqrt(mean_square + 1e-06)).astype(BF16)


def steps(name, size, step):
    block = min(BLOCKS[name], size)

    def body(i, carry):
        step(pl.ds(pl.multiple_of(i * block, block), block))
        return carry

    lax.fori_loop(0, size // block, body, 0)


def block_of(name, size):
    return min(BLOCKS[name], size // 2)


def pipelined(n, fill, work, subs=1):
    def both(i, slot):
        for m in range(subs):
            fill(i, slot, m)
            work(i - 1, 1 - slot, m)

    def body(i, carry):
        both(2 * i + 1, 1)
        both(2 * i + 2, 0)
        return carry

    for m in range(subs):
        fill(0, 0, m)
    if n <= 4:
        for i in range(1, n - 1):
            both(i, i % 2)
    else:
        lax.fori_loop(0, n // 2 - 1, body, 0)
    both(n - 1, 1)
    for m in range(subs):
        work(n - 1, 1, m)


def part(i, size):
    return pl.ds(i * size if isinstance(i, int) else pl.multiple_of(i * size, size), size)


def similarity(a, b):
    return lax.dot_general(a, b, (((1,), (1,)), ((), ())), preferred_element_type=F32)


def sublane_sums(block):
    return jnp.sum(block.reshape(block.shape[0] // 8, 8, block.shape[1]), axis=0)


def lane_sums(block):
    return sum(block[:, i : i + 128] for i in range(0, block.shape[1], 128))


def own_codes(proto_ref, token_ref, code_ref, centre_ref, column_ref, *, scale):
    own = token_ref.shape[0]
    tok = normalize(token_ref[...])

    def step(at):
        centre = normalize(proto_ref[at, :])
        centre_ref[at, :] = centre
        code = jnp.exp2(similarity(centre, tok) * scale)
        code_ref[at, :own] = code
        column_ref[at, :] = lane_sums(code)

    steps("own", proto_ref.shape[0], step)


def first_pass(*refs, parts, by_core, scale, total):
    (_, centre_ref, column_ref), token_refs = refs[:3], refs[3 : 3 + parts]
    code_ref, out_ref, tok, acc, columns = refs[3 + parts :]
    n = token_refs[0].shape[0]
    if by_core:
        core = lax.rem(lax.axis_index("proto"), 2)
        far, near, swapped_far, swapped_near = token_refs
        tok[part(core, n), :] = normalize(near[...])
        tok[part(1 - core, n), :] = normalize(swapped_near[...])
        for c, t in enumerate((far, swapped_far)):

            @pl.when(core == c)
            def _():
                tok[2 * n :, :] = normalize(t[...])

    else:
        for i, t in enumerate(token_refs[::-1]):
            tok[i * n : (i + 1) * n, :] = normalize(t[...])
    acc[...] = jnp.zeros_like(acc)
    block = block_of("first", centre_ref.shape[0])

    size = block // SUBS["first"]

    def rows(i, m):
        start = i * block + m * size
        return pl.ds(start if isinstance(i, int) else pl.multiple_of(start, size), size)

    def fill(i, slot, m):
        at = rows(i, m)
        code = jnp.exp2(similarity(centre_ref[at, :], tok[...]) * scale)
        code_ref[at, n:] = code
        columns[at, :] = column_ref[at, :] + lane_sums(code)

    def work(i, slot, m):
        at = rows(i, m)
        factor = 1.0 / (total * jnp.sum(columns[at, :], axis=1, keepdims=True))
        acc[...] += sublane_sums(code_ref[at, :] * factor)

    pipelined(centre_ref.shape[0] // block, fill, work, SUBS["first"])
    out_ref[...] = jnp.sum(acc[...], axis=0, keepdims=True)


def denominators(_, centre_ref, token_ref, code_ref, tok_ref, out_ref, acc, *, scale):
    tok_ref[...] = normalize(token_ref[...])
    acc[...] = jnp.zeros_like(acc)

    def step(at):
        acc[...] += sublane_sums(jnp.exp2(similarity(centre_ref[at, :], tok_ref[...]) * scale))

    steps("den", centre_ref.shape[0], step)
    out_ref[...] = jnp.sum(acc[...], axis=0, keepdims=True)


def term_sum(refs):
    return functools.reduce(lambda a, b: a + b, [r[...] for r in refs])


def middle_pass(*refs, parts, total):
    den_ref, (code_ref, out_ref, acc) = refs[1 + parts], refs[2 + parts :]
    token_scale = 1.0 / term_sum(refs[1 : 1 + parts])
    acc[...] = jnp.zeros_like(acc)

    def step(at):
        code = code_ref[at, :]
        factor = 1.0 / (total * jnp.sum(code * token_scale, axis=1, keepdims=True))
        acc[...] += sublane_sums(code * factor)

    steps("middle", code_ref.shape[0], step)
    tokens = acc.shape[1]
    out_ref[:, :tokens] = jnp.sum(acc[...], axis=0, keepdims=True)
    out_ref[:, tokens:] = den_ref[...]


def last_pass(*refs, parts, total):
    tok_ref, (code_ref, out_ref, weight_ref, pack_ref, acc) = refs[1 + parts], refs[2 + parts :]
    tokens, own = acc.shape[1], tok_ref.shape[0]
    sums = term_sum(refs[1 : 1 + parts])
    token_scale = 1.0 / sums[:, :tokens]
    weight = total / sums[:, tokens:]
    weight_ref[...] = weight
    pack_ref[:own, :] = tok_ref[...]
    lines = [weight[:, i : i + 128] for i in range(0, own, 128)]
    pieces, rest = [], jnp.concatenate(lines, axis=0)
    for _ in range(SPLIT):
        piece = rest.astype(BF16).astype(F32)
        pieces.append(piece)
        rest = rest - piece
    rows = SPLIT * len(lines)
    pad = -rows % TILE
    pack_ref[own:, :] = jnp.concatenate(pieces + [jnp.zeros((pad, 128), F32)], axis=0).astype(BF16)
    acc[...] = jnp.zeros_like(acc)

    def step(at):
        code = code_ref[at, :]
        factor = 1.0 / (total * jnp.sum(code * token_scale, axis=1, keepdims=True))
        scaled = code * factor
        code_ref[at, :] = scaled
        acc[...] += sublane_sums(scaled)

    steps("middle", code_ref.shape[0], step)
    out_ref[...] = jnp.sum(acc[...], axis=0, keepdims=True)


def logit(centre, tok, code, token_scale, weight, scale):
    pred = jnp.exp2(similarity(centre, tok) * scale) * weight
    return (pred - code * token_scale).astype(BF16)


def token_part(*refs, parts, scale, total):
    centre_ref, tok_ref, weight_ref = refs[1:4]
    code_ref, mine_ref, other_ref, scale_ref, logit_ref, acc = refs[4 + parts :]
    own = tok_ref.shape[0]
    core = lax.rem(lax.axis_index("proto"), 2)
    scale_ref[...] = total / term_sum(refs[4 : 4 + parts])
    acc[...] = jnp.zeros_like(acc)
    block = block_of("token", code_ref.shape[0])

    def fill(i, slot, m):
        at = part(i, block)
        for c in range(0, own, CHUNK):
            c = slice(c, min(c + CHUNK, own))
            logit_ref[at, c] = logit(
                centre_ref[at, :], tok_ref[c, :], code_ref[at, c], scale_ref[:, c], weight_ref[:, c], scale
            )

    def work(i, slot, m):
        at = part(i, block)
        acc[...] += lax.dot_general(
            centre_ref[at, :], logit_ref[at, :], (((0,), (0,)), ((), ())), preferred_element_type=F32
        )

    pipelined(code_ref.shape[0] // block, fill, work)
    acc[...] = acc[...] * total ** (-0.5)
    half = own // 2
    for c in range(2):

        @pl.when(core == c)
        def _():
            mine_ref[...] = acc[:, c * half : (c + 1) * half].T
            other_ref[...] = acc[:, (1 - c) * half : (2 - c) * half].T


def proto_part(*refs, parts, scale):
    (code_ref, centre_ref, tok_ref, scale_ref, logit_ref), packs = refs[:5], refs[5 : 5 + parts]
    out_ref, tok, weight, *slots = refs[5 + parts :]
    tokens, own = code_ref.shape[1], tok_ref.shape[0]
    for i, pack in enumerate(packs[::-1]):
        tok[i * own : (i + 1) * own, :] = pack[:own, :]
        pieces = pack[own:, :].astype(F32)
        count = own // 128
        lines = sum(pieces[j * count : (j + 1) * count, :] for j in range(SPLIT))
        for j in range(count):
            at = i * own + j * 128
            weight[:, at : at + 128] = lines[j : j + 1, :]

    subs = SUBS["proto"]
    size = code_ref.shape[0] // subs

    def fill(i, slot, m):
        at = part(i, CHUNK)
        c = pl.ds(pl.multiple_of(own + i * CHUNK, 128), CHUNK)
        r = slice(m * size, (m + 1) * size)
        slots[slot][r, :] = logit(
            centre_ref[r, :], tok[at, :], code_ref[r, c], scale_ref[:, c], weight[:, at], scale
        )

    def work(i, slot, m):
        r = slice(m * size, (m + 1) * size)
        out_ref[r, :] += jnp.dot(slots[slot][r, :], tok[part(i, CHUNK), :], preferred_element_type=F32)

    out_ref[...] = jnp.dot(logit_ref[...], tok_ref[...], preferred_element_type=F32)
    pipelined(parts * own // CHUNK, fill, work, subs)
    out_ref[...] = out_ref[...] * tokens ** (-0.5)


def swapped(x, axis, mask):
    return lax.ppermute(x, axis, [(i, i ^ mask) for i in range(lax.axis_size(axis))])


def others_of(x, axis):
    return [swapped(x, axis, m) for m in range(lax.axis_size(axis) - 1, 0, -1)]


def others_by_core(x):
    dp, proto = lax.axis_size("dp"), lax.axis_size("proto")

    def fetched(masks):
        pairs = [
            (i * proto + j, (i ^ masks[j % 2]) * proto + j) for i in range(dp) for j in range(proto)
        ]
        return lax.ppermute(x, ("dp", "proto"), pairs)

    return [fetched((3, 0)), fetched((1, 2))]


def proto_terms(x):
    n = lax.axis_size("proto")
    x = x + swapped(x, "proto", 1)
    terms, unit = [x], 2
    while unit < n:
        group = min(4, n // unit)
        if unit > 2:
            terms = [sum(terms)]
        terms = [terms[0]] + [swapped(terms[0], "proto", unit * m) for m in range(group - 1, 0, -1)]
        unit *= group
    return terms


def chip_sum(x):
    n, unit = lax.axis_size("proto"), 2
    while unit < n:
        group = min(4, n // unit)
        x = sum([swapped(x, "proto", unit * m) for m in range(group - 1, 0, -1)], x)
        unit *= group
    return x


def local(first_view, alternate_augmentation, prototypes):
    own, d = first_view.shape
    k = prototypes.shape[0]
    tokens = own * lax.axis_size("dp")
    total = float(k * lax.axis_size("proto"))
    log2e = math.log2(math.e)
    code_scale = log2e / d / CODE_TEMP
    pred_scale = log2e / d / PRED_TEMP
    acc = pltpu.VMEM((8, tokens), F32)

    by_core = lax.axis_size("dp") == 4
    views = others_by_core(first_view) if by_core else others_of(first_view, "dp")
    code, centres, columns = run(
        functools.partial(own_codes, scale=code_scale),
        [shape(k, tokens), shape(k, d, dtype=BF16), shape(k, 128)],
        [prototypes, first_view],
        [],
        keep=(0, 1, 2),
        us=3,
    )
    parts = lax.axis_size("dp") - 1
    if by_core:
        *views, columns = lax.optimization_barrier((*views, columns))
        views = views + [swapped(v, "proto", 1) for v in views]
    code, sums = run(
        functools.partial(
            first_pass, parts=len(views), by_core=by_core, scale=code_scale, total=total
        ),
        [shape(1, tokens)],
        [code, centres, columns] + views,
        [pltpu.VMEM((tokens - own, d), BF16), acc, pltpu.VMEM((k, 128), F32)],
        resident=list(range(1, 3 + len(views))),
        keep=[0],
        thread=True,
        us=7,
    )
    terms = proto_terms(sums)
    code, tok, den = run(
        functools.partial(denominators, scale=pred_scale),
        [shape(own, d, dtype=BF16), shape(1, own)],
        [code, centres, alternate_augmentation],
        [pltpu.VMEM((8, own), F32)],
        resident=[1],
        keep=[0, 1],
        thread=True,
        us=2,
    )
    code, sums = run(
        functools.partial(middle_pass, parts=len(terms), total=total),
        [shape(1, tokens + own)],
        [code] + terms + [den],
        [acc],
        resident=list(range(1, 2 + len(terms))),
        keep=[0],
        thread=True,
        us=5,
    )
    terms = proto_terms(sums)
    terms = terms[:1] + terms[2:] + terms[1:2]
    pack_rows = own + -(-SPLIT * own // 128 // TILE) * TILE
    code, sums, weight, pack = run(
        functools.partial(last_pass, parts=len(terms), total=total),
        [shape(1, tokens), shape(1, own), shape(pack_rows, d, dtype=BF16)],
        [code] + terms + [tok],
        [acc],
        resident=list(range(1, 2 + len(terms))),
        keep=[0, 1, 2],
        thread=True,
        us=5,
    )
    terms = proto_terms(sums)
    packs = others_of(pack, "dp")
    code, mine, other, token_scale, logits = run(
        functools.partial(token_part, parts=len(terms), scale=pred_scale, total=total),
        [shape(own // 2, d), shape(own // 2, d), shape(1, tokens), shape(k, own, dtype=BF16)],
        [code, centres, tok, weight] + terms,
        [pltpu.VMEM((d, own), F32)],
        resident=list(range(1, 4 + len(terms))),
        keep=[0, 1, 2, 3],
        thread=True,
        us=4,
    )
    mine = chip_sum(mine + swapped(other, "proto", 1))
    (proto_grad,) = run(
        functools.partial(proto_part, parts=parts, scale=pred_scale),
        [shape(k, d)],
        [code, centres, tok, token_scale, logits] + packs,
        [pltpu.VMEM((tokens - own, d), BF16), pltpu.VMEM((1, tokens - own), F32)]
        + [pltpu.VMEM((k, CHUNK), BF16)] * 2,
        resident=range(5 + parts),
        us=10,
    )
    mine, proto_grad = lax.optimization_barrier((mine, proto_grad))
    other = swapped(mine, "proto", 1)
    first = lax.rem(lax.axis_index("proto"), 2) == 0
    token_grad = jnp.where(
        first, jnp.concatenate([mine, other]), jnp.concatenate([other, mine])
    )
    return proto_grad, token_grad


def solution(mesh):
    return jax.shard_map(
        local,
        mesh=mesh,
        in_specs=(P("dp", None), P("dp", None), P("proto", None)),
        out_specs=(P("proto", None), P("dp", None)),
        check_vma=False,
    )
```

```python
import functools
import math

import jax
import jax.numpy as jnp
from jax import lax
from jax.experimental import pallas as pl
from jax.experimental.pallas import tpu as pltpu
from jax.sharding import PartitionSpec as P

CODE_TEMP = 0.05
PRED_TEMP = 0.1
F32 = jnp.float32
BF16 = jnp.bfloat16
VMEM_LIMIT = 20 << 20
CHUNK = 256
BLOCKS = {"own": 2048, "first": 1024, "den": 2048, "middle": 512, "token": 2048}
SUBS = {"first": 1, "proto": 1}
COPIES = 4
SPLIT = 3
TILE = 16


def vmem_spec():
    return pl.BlockSpec(memory_space=pltpu.VMEM)


def shape(*dims, dtype=F32):
    return jax.ShapeDtypeStruct(dims, dtype)


def run(body, outs, args, scratch, resident=(), keep=(), us=1.0, thread=False, copied=()):
    if thread:
        outs = [shape(*args[0].shape, dtype=args[0].dtype)] + outs
        keep = [0] + [i + 1 for i in keep]
        resident = [0] + list(resident)
    return pl.pallas_call(
        body,
        out_shape=tuple(pltpu.VMEM(s.shape, s.dtype) if i in keep else s for i, s in enumerate(outs)),
        in_specs=[vmem_spec()] * len(args),
        out_specs=tuple(
            pl.BlockSpec(memory_space=pl.ANY) if i in copied else vmem_spec() for i in range(len(outs))
        ),
        scratch_shapes=scratch,
        input_output_aliases={0: 0} if thread else {},
        compiler_params=pltpu.CompilerParams(vmem_limit_bytes=VMEM_LIMIT),
        cost_estimate=pl.CostEstimate(flops=int(us * 1e9), bytes_accessed=1 << 20, transcendentals=0),
    )(
        *[
            pltpu.with_memory_space_constraint(a, pltpu.VMEM) if i in resident else a
            for i, a in enumerate(args)
        ]
    )


def normalize(values):
    floats = values.astype(F32)
    mean_square = jnp.mean(floats * floats, axis=-1, keepdims=True)
    return (floats * lax.rsqrt(mean_square + 1e-06)).astype(BF16)


def steps(name, size, step):
    block = min(BLOCKS[name], size)

    def body(i, carry):
        step(pl.ds(pl.multiple_of(i * block, block), block))
        return carry

    lax.fori_loop(0, size // block, body, 0)


def block_of(name, size):
    return min(BLOCKS[name], size // 2)


def pipelined(n, fill, work, subs=1, end=None):
    def both(i, slot):
        for m in range(subs):
            fill(i, slot, m)
            work(i - 1, 1 - slot, m)

    def body(i, carry):
        both(2 * i + 1, 1)
        both(2 * i + 2, 0)
        return carry

    for m in range(subs):
        fill(0, 0, m)
    if n <= 4:
        for i in range(1, n - 1):
            both(i, i % 2)
    else:
        lax.fori_loop(0, n // 2 - 1, body, 0)
    both(n - 1, 1)
    if end is not None:
        end()
    else:
        for m in range(subs):
            work(n - 1, 1, m)


def part(i, size):
    return pl.ds(i * size if isinstance(i, int) else pl.multiple_of(i * size, size), size)


def similarity(a, b):
    return lax.dot_general(a, b, (((1,), (1,)), ((), ())), preferred_element_type=F32)


def sublane_sums(block):
    return jnp.sum(block.reshape(block.shape[0] // 8, 8, block.shape[1]), axis=0)


def lane_sums(block):
    return sum(block[:, i : i + 128] for i in range(0, block.shape[1], 128))


def own_codes(proto_ref, token_ref, code_ref, centre_ref, column_ref, *, scale):
    own = token_ref.shape[0]
    tok = normalize(token_ref[...])

    def step(at):
        centre = normalize(proto_ref[at, :])
        centre_ref[at, :] = centre
        code = jnp.exp2(similarity(centre, tok) * scale)
        code_ref[at, :own] = code
        column_ref[at, :] = lane_sums(code)

    steps("own", proto_ref.shape[0], step)


def more_codes(_, centre_ref, column_ref, token_ref, code_ref, out_ref, *, scale):
    own = token_ref.shape[0]
    tok = normalize(token_ref[...])

    def step(at):
        code = jnp.exp2(similarity(centre_ref[at, :], tok) * scale)
        code_ref[at, own : 2 * own] = code
        out_ref[at, :] = column_ref[at, :] + lane_sums(code)

    steps("own", centre_ref.shape[0], step)


def first_pass(*refs, parts, scale, total):
    (_, centre_ref, column_ref), token_refs = refs[:3], refs[3 : 3 + parts]
    code_ref, out_ref, tok, acc, columns = refs[3 + parts :]
    n = token_refs[0].shape[0]
    done = code_ref.shape[1] - parts * n
    for i, t in enumerate(token_refs):
        tok[i * n : (i + 1) * n, :] = normalize(t[...])
    acc[...] = jnp.zeros_like(acc)
    block = block_of("first", centre_ref.shape[0])

    size = block // SUBS["first"]

    def rows(i, m):
        start = i * block + m * size
        return pl.ds(start if isinstance(i, int) else pl.multiple_of(start, size), size)

    def fill(i, slot, m):
        at = rows(i, m)
        code = jnp.exp2(similarity(centre_ref[at, :], tok[...]) * scale)
        code_ref[at, done:] = code
        columns[at, :] = column_ref[at, :] + lane_sums(code)

    def work(i, slot, m):
        at = rows(i, m)
        factor = 1.0 / (total * jnp.sum(columns[at, :], axis=1, keepdims=True))
        acc[...] += sublane_sums(code_ref[at, :] * factor)

    pipelined(centre_ref.shape[0] // block, fill, work, SUBS["first"])
    out_ref[...] = jnp.sum(acc[...], axis=0, keepdims=True)


def denominators(_, centre_ref, token_ref, code_ref, tok_ref, out_ref, acc, *, scale):
    tok_ref[...] = normalize(token_ref[...])
    acc[...] = jnp.zeros_like(acc)

    def step(at):
        acc[...] += sublane_sums(jnp.exp2(similarity(centre_ref[at, :], tok_ref[...]) * scale))

    steps("den", centre_ref.shape[0], step)
    out_ref[...] = jnp.sum(acc[...], axis=0, keepdims=True)


def term_sum(refs):
    return functools.reduce(lambda a, b: a + b, [r[...] for r in refs])


def middle_pass(*refs, parts, total):
    den_ref, (code_ref, out_ref, acc) = refs[1 + parts], refs[2 + parts :]
    token_scale = 1.0 / term_sum(refs[1 : 1 + parts])
    acc[...] = jnp.zeros_like(acc)

    def step(at):
        code = code_ref[at, :]
        factor = 1.0 / (total * jnp.sum(code * token_scale, axis=1, keepdims=True))
        acc[...] += sublane_sums(code * factor)

    steps("middle", code_ref.shape[0], step)
    tokens = acc.shape[1]
    out_ref[:, :tokens] = jnp.sum(acc[...], axis=0, keepdims=True)
    out_ref[:, tokens:] = den_ref[...]


def last_pass(*refs, parts, total):
    tok_ref, (code_ref, out_ref, weight_ref, pack_ref, acc) = refs[1 + parts], refs[2 + parts :]
    tokens, own = acc.shape[1], tok_ref.shape[0]
    sums = term_sum(refs[1 : 1 + parts])
    token_scale = 1.0 / sums[:, :tokens]
    weight = total / sums[:, tokens:]
    weight_ref[...] = weight
    pack_ref[:own, :] = tok_ref[...]
    lines = [weight[:, i : i + 128] for i in range(0, own, 128)]
    pieces, rest = [], jnp.concatenate(lines, axis=0)
    for _ in range(SPLIT):
        piece = rest.astype(BF16).astype(F32)
        pieces.append(piece)
        rest = rest - piece
    rows = SPLIT * len(lines)
    pad = -rows % TILE
    pack_ref[own:, :] = jnp.concatenate(pieces + [jnp.zeros((pad, 128), F32)], axis=0).astype(BF16)
    acc[...] = jnp.zeros_like(acc)

    def step(at):
        code = code_ref[at, :]
        factor = 1.0 / (total * jnp.sum(code * token_scale, axis=1, keepdims=True))
        scaled = code * factor
        code_ref[at, :] = scaled
        acc[...] += sublane_sums(scaled)

    steps("middle", code_ref.shape[0], step)
    out_ref[...] = jnp.sum(acc[...], axis=0, keepdims=True)


def logit(centre, tok, code, token_scale, weight, scale):
    pred = jnp.exp2(similarity(centre, tok) * scale) * weight
    return (pred - code * token_scale).astype(BF16)


def token_part(*refs, parts, scale, total):
    centre_ref, tok_ref, weight_ref = refs[1:4]
    code_ref, mine_ref, other_ref, scale_ref, logit_ref, acc = refs[4 + parts :]
    own = tok_ref.shape[0]
    core = lax.rem(lax.axis_index("proto"), 2)
    scale_ref[...] = total / term_sum(refs[4 : 4 + parts])
    acc[...] = jnp.zeros_like(acc)
    block = block_of("token", code_ref.shape[0])

    def fill(i, slot, m):
        at = part(i, block)
        for c in range(0, own, CHUNK):
            c = slice(c, min(c + CHUNK, own))
            logit_ref[at, c] = logit(
                centre_ref[at, :], tok_ref[c, :], code_ref[at, c], scale_ref[:, c], weight_ref[:, c], scale
            )

    def work(i, slot, m):
        at = part(i, block)
        acc[...] += lax.dot_general(
            centre_ref[at, :], logit_ref[at, :], (((0,), (0,)), ((), ())), preferred_element_type=F32
        )

    pipelined(code_ref.shape[0] // block, fill, work)
    acc[...] = acc[...] * total ** (-0.5)
    half = own // 2
    for c in range(2):

        @pl.when(core == c)
        def _():
            mine_ref[...] = acc[:, c * half : (c + 1) * half].T
            other_ref[...] = acc[:, (1 - c) * half : (2 - c) * half].T


def proto_part(*refs, parts, scale):
    (code_ref, centre_ref, tok_ref, scale_ref, logit_ref), packs = refs[:5], refs[5 : 5 + parts]
    result_ref, tok, weight, out_ref, sems, *slots = refs[5 + parts :]
    tokens, own = code_ref.shape[1], tok_ref.shape[0]
    for i, pack in enumerate(packs):
        tok[i * own : (i + 1) * own, :] = pack[:own, :]
        pieces = pack[own:, :].astype(F32)
        count = own // 128
        lines = sum(pieces[j * count : (j + 1) * count, :] for j in range(SPLIT))
        for j in range(count):
            at = i * own + j * 128
            weight[:, at : at + 128] = lines[j : j + 1, :]

    subs = SUBS["proto"]
    size = code_ref.shape[0] // subs

    def fill(i, slot, m):
        at = part(i, CHUNK)
        c = pl.ds(pl.multiple_of(own + i * CHUNK, 128), CHUNK)
        r = slice(m * size, (m + 1) * size)
        slots[slot][r, :] = logit(
            centre_ref[r, :], tok[at, :], code_ref[r, c], scale_ref[:, c], weight[:, at], scale
        )

    def work(i, slot, m):
        r = slice(m * size, (m + 1) * size)
        out_ref[r, :] += jnp.dot(slots[slot][r, :], tok[part(i, CHUNK), :], preferred_element_type=F32)

    out_ref[...] = jnp.dot(logit_ref[...], tok_ref[...], preferred_element_type=F32)
    count = parts * own // CHUNK
    copies = []

    def end():
        rows = out_ref.shape[0] // COPIES
        for j in range(COPIES):
            r = slice(j * rows, (j + 1) * rows)
            last = jnp.dot(slots[1][r, :], tok[part(count - 1, CHUNK), :], preferred_element_type=F32)
            out_ref[r, :] = (out_ref[r, :] + last) * tokens ** (-0.5)
            copies.append(
                pltpu.make_async_copy(out_ref.at[pl.ds(j * rows, rows)], result_ref.at[pl.ds(j * rows, rows)], sems.at[j])
            )
            copies[-1].start()

    pipelined(count, fill, work, subs, end)
    for c in copies:
        c.wait()


def swapped(x, axis, mask):
    return lax.ppermute(x, axis, [(i, i ^ mask) for i in range(lax.axis_size(axis))])


def others_of(x, axis):
    return [swapped(x, axis, m) for m in range(lax.axis_size(axis) - 1, 0, -1)]


def proto_terms(x):
    n = lax.axis_size("proto")
    x = x + swapped(x, "proto", 1)
    terms, unit = [x], 2
    while unit < n:
        group = min(4, n // unit)
        if unit > 2:
            terms = [sum(terms)]
        terms = [terms[0]] + [swapped(terms[0], "proto", unit * m) for m in range(group - 1, 0, -1)]
        unit *= group
    return terms


def chip_sum(x):
    n, unit = lax.axis_size("proto"), 2
    while unit < n:
        group = min(4, n // unit)
        x = sum([swapped(x, "proto", unit * m) for m in range(group - 1, 0, -1)], x)
        unit *= group
    return x


def local(first_view, alternate_augmentation, prototypes):
    own, d = first_view.shape
    k = prototypes.shape[0]
    tokens = own * lax.axis_size("dp")
    total = float(k * lax.axis_size("proto"))
    log2e = math.log2(math.e)
    code_scale = log2e / d / CODE_TEMP
    pred_scale = log2e / d / PRED_TEMP
    acc = pltpu.VMEM((8, tokens), F32)

    views = others_of(first_view, "dp")
    code, centres, columns = run(
        functools.partial(own_codes, scale=code_scale),
        [shape(k, tokens), shape(k, d, dtype=BF16), shape(k, 128)],
        [prototypes, first_view],
        [],
        keep=(0, 1, 2),
        us=3,
    )
    parts = len(views)
    code, columns = run(
        functools.partial(more_codes, scale=code_scale),
        [shape(k, 128)],
        [code, centres, columns, views[0]],
        [],
        resident=[1, 2, 3],
        keep=[0],
        thread=True,
        us=2,
    )
    views = views[1:]
    code, sums = run(
        functools.partial(first_pass, parts=len(views), scale=code_scale, total=total),
        [shape(1, tokens)],
        [code, centres, columns] + views,
        [pltpu.VMEM((len(views) * own, d), BF16), acc, pltpu.VMEM((k, 128), F32)],
        resident=list(range(1, 3 + len(views))),
        keep=[0],
        thread=True,
        us=7,
    )
    terms = proto_terms(sums)
    code, tok, den = run(
        functools.partial(denominators, scale=pred_scale),
        [shape(own, d, dtype=BF16), shape(1, own)],
        [code, centres, alternate_augmentation],
        [pltpu.VMEM((8, own), F32)],
        resident=[1],
        keep=[0, 1],
        thread=True,
        us=2,
    )
    code, sums = run(
        functools.partial(middle_pass, parts=len(terms), total=total),
        [shape(1, tokens + own)],
        [code] + terms + [den],
        [acc],
        resident=list(range(1, 2 + len(terms))),
        keep=[0],
        thread=True,
        us=5,
    )
    terms = proto_terms(sums)
    terms = terms[:1] + terms[2:] + terms[1:2]
    pack_rows = own + -(-SPLIT * own // 128 // TILE) * TILE
    code, sums, weight, pack = run(
        functools.partial(last_pass, parts=len(terms), total=total),
        [shape(1, tokens), shape(1, own), shape(pack_rows, d, dtype=BF16)],
        [code] + terms + [tok],
        [acc],
        resident=list(range(1, 2 + len(terms))),
        keep=[0, 1, 2],
        thread=True,
        us=5,
    )
    terms = proto_terms(sums)
    packs = others_of(pack, "dp")
    code, mine, other, token_scale, logits = run(
        functools.partial(token_part, parts=len(terms), scale=pred_scale, total=total),
        [shape(own // 2, d), shape(own // 2, d), shape(1, tokens), shape(k, own, dtype=BF16)],
        [code, centres, tok, weight] + terms,
        [pltpu.VMEM((d, own), F32)],
        resident=list(range(1, 4 + len(terms))),
        keep=[0, 1, 2, 3],
        thread=True,
        us=4,
    )
    mine = chip_sum(mine + swapped(other, "proto", 1))
    (proto_grad,) = run(
        functools.partial(proto_part, parts=parts, scale=pred_scale),
        [shape(k, d)],
        [code, centres, tok, token_scale, logits] + packs,
        [pltpu.VMEM((tokens - own, d), BF16), pltpu.VMEM((1, tokens - own), F32)]
        + [pltpu.VMEM((k, d), F32), pltpu.SemaphoreType.DMA((COPIES,))]
        + [pltpu.VMEM((k, CHUNK), BF16)] * 2,
        resident=range(5 + parts),
        copied=[0],
        us=10,
    )
    mine, proto_grad = lax.optimization_barrier((mine, proto_grad))
    other = swapped(mine, "proto", 1)
    first = lax.rem(lax.axis_index("proto"), 2) == 0
    token_grad = jnp.where(
        first, jnp.concatenate([mine, other]), jnp.concatenate([other, mine])
    )
    return proto_grad, token_grad


def solution(mesh):
    return jax.shard_map(
        local,
        mesh=mesh,
        in_specs=(P("dp", None), P("dp", None), P("proto", None)),
        out_specs=(P("proto", None), P("dp", None)),
        check_vma=False,
    )
```

```python
import functools
import math

import jax
import jax.numpy as jnp
from jax import lax
from jax.experimental import pallas as pl
from jax.experimental.pallas import tpu as pltpu
from jax.sharding import PartitionSpec as P

CODE_TEMP = 0.05
PRED_TEMP = 0.1
F32 = jnp.float32
BF16 = jnp.bfloat16
VMEM_LIMIT = 20 << 20
CHUNK = 256
BLOCKS = {"own": 2048, "first": 1024, "den": 2048, "middle": 512, "token": 2048}
SUBS = {"first": 1, "proto": 1}
COPIES = 4
SPLIT = 3
TILE = 16


def vmem_spec():
    return pl.BlockSpec(memory_space=pltpu.VMEM)


def shape(*dims, dtype=F32):
    return jax.ShapeDtypeStruct(dims, dtype)


def run(body, outs, args, scratch, resident=(), keep=(), us=1.0, thread=False, copied=()):
    if thread:
        outs = [shape(*args[0].shape, dtype=args[0].dtype)] + outs
        keep = [0] + [i + 1 for i in keep]
        resident = [0] + list(resident)
    return pl.pallas_call(
        body,
        out_shape=tuple(pltpu.VMEM(s.shape, s.dtype) if i in keep else s for i, s in enumerate(outs)),
        in_specs=[vmem_spec()] * len(args),
        out_specs=tuple(
            pl.BlockSpec(memory_space=pl.ANY) if i in copied else vmem_spec() for i in range(len(outs))
        ),
        scratch_shapes=scratch,
        input_output_aliases={0: 0} if thread else {},
        compiler_params=pltpu.CompilerParams(vmem_limit_bytes=VMEM_LIMIT),
        cost_estimate=pl.CostEstimate(flops=int(us * 1e9), bytes_accessed=1 << 20, transcendentals=0),
    )(
        *[
            pltpu.with_memory_space_constraint(a, pltpu.VMEM) if i in resident else a
            for i, a in enumerate(args)
        ]
    )


def normalize(values):
    floats = values.astype(F32)
    mean_square = jnp.mean(floats * floats, axis=-1, keepdims=True)
    return (floats * lax.rsqrt(mean_square + 1e-06)).astype(BF16)


def steps(name, size, step):
    block = min(BLOCKS[name], size)

    def body(i, carry):
        step(pl.ds(pl.multiple_of(i * block, block), block))
        return carry

    lax.fori_loop(0, size // block, body, 0)


def block_of(name, size):
    return min(BLOCKS[name], size // 2)


def pipelined(n, fill, work, subs=1, end=None):
    def both(i, slot):
        for m in range(subs):
            fill(i, slot, m)
            work(i - 1, 1 - slot, m)

    def body(i, carry):
        both(2 * i + 1, 1)
        both(2 * i + 2, 0)
        return carry

    for m in range(subs):
        fill(0, 0, m)
    if n <= 4:
        for i in range(1, n - 1):
            both(i, i % 2)
    else:
        lax.fori_loop(0, n // 2 - 1, body, 0)
    both(n - 1, 1)
    if end is not None:
        end()
    else:
        for m in range(subs):
            work(n - 1, 1, m)


def part(i, size):
    return pl.ds(i * size if isinstance(i, int) else pl.multiple_of(i * size, size), size)


def similarity(a, b):
    return lax.dot_general(a, b, (((1,), (1,)), ((), ())), preferred_element_type=F32)


def sublane_sums(block):
    return jnp.sum(block.reshape(block.shape[0] // 8, 8, block.shape[1]), axis=0)


def lane_sums(block):
    return sum(block[:, i : i + 128] for i in range(0, block.shape[1], 128))


def own_codes(proto_ref, token_ref, code_ref, centre_ref, column_ref, *, scale):
    own = token_ref.shape[0]
    tok = normalize(token_ref[...])

    def step(at):
        centre = normalize(proto_ref[at, :])
        centre_ref[at, :] = centre
        code = jnp.exp2(similarity(centre, tok) * scale)
        code_ref[at, :own] = code
        column_ref[at, :] = lane_sums(code)

    steps("own", proto_ref.shape[0], step)


def more_codes(_, centre_ref, column_ref, token_ref, code_ref, out_ref, *, scale):
    own = token_ref.shape[0]
    tok = normalize(token_ref[...])

    def step(at):
        code = jnp.exp2(similarity(centre_ref[at, :], tok) * scale)
        code_ref[at, own : 2 * own] = code
        out_ref[at, :] = column_ref[at, :] + lane_sums(code)

    steps("own", centre_ref.shape[0], step)


def first_pass(*refs, parts, scale, total):
    (_, centre_ref, column_ref), token_refs = refs[:3], refs[3 : 3 + parts]
    code_ref, out_ref, tok, acc, columns = refs[3 + parts :]
    n = token_refs[0].shape[0]
    done = code_ref.shape[1] - parts * n
    for i, t in enumerate(token_refs):
        tok[i * n : (i + 1) * n, :] = normalize(t[...])
    acc[...] = jnp.zeros_like(acc)
    block = block_of("first", centre_ref.shape[0])

    size = block // SUBS["first"]

    def rows(i, m):
        start = i * block + m * size
        return pl.ds(start if isinstance(i, int) else pl.multiple_of(start, size), size)

    def fill(i, slot, m):
        at = rows(i, m)
        code = jnp.exp2(similarity(centre_ref[at, :], tok[...]) * scale)
        code_ref[at, done:] = code
        columns[at, :] = column_ref[at, :] + lane_sums(code)

    def work(i, slot, m):
        at = rows(i, m)
        factor = 1.0 / (total * jnp.sum(columns[at, :], axis=1, keepdims=True))
        acc[...] += sublane_sums(code_ref[at, :] * factor)

    pipelined(centre_ref.shape[0] // block, fill, work, SUBS["first"])
    out_ref[...] = jnp.sum(acc[...], axis=0, keepdims=True)


def denominators(_, centre_ref, token_ref, code_ref, tok_ref, out_ref, acc, *, scale):
    tok_ref[...] = normalize(token_ref[...])
    acc[...] = jnp.zeros_like(acc)

    def step(at):
        acc[...] += sublane_sums(jnp.exp2(similarity(centre_ref[at, :], tok_ref[...]) * scale))

    steps("den", centre_ref.shape[0], step)
    out_ref[...] = jnp.sum(acc[...], axis=0, keepdims=True)


def term_sum(refs):
    return functools.reduce(lambda a, b: a + b, [r[...] for r in refs])


def middle_pass(*refs, parts, total):
    den_ref, (code_ref, out_ref, acc) = refs[1 + parts], refs[2 + parts :]
    token_scale = 1.0 / term_sum(refs[1 : 1 + parts])
    acc[...] = jnp.zeros_like(acc)

    def step(at):
        code = code_ref[at, :]
        factor = 1.0 / (total * jnp.sum(code * token_scale, axis=1, keepdims=True))
        acc[...] += sublane_sums(code * factor)

    steps("middle", code_ref.shape[0], step)
    tokens = acc.shape[1]
    out_ref[:, :tokens] = jnp.sum(acc[...], axis=0, keepdims=True)
    out_ref[:, tokens:] = den_ref[...]


def last_pass(*refs, parts, total):
    tok_ref, (code_ref, out_ref, weight_ref, pack_ref, acc) = refs[1 + parts], refs[2 + parts :]
    tokens, own = acc.shape[1], tok_ref.shape[0]
    sums = term_sum(refs[1 : 1 + parts])
    token_scale = 1.0 / sums[:, :tokens]
    weight = total / sums[:, tokens:]
    weight_ref[...] = weight
    pack_ref[:own, :] = tok_ref[...]
    lines = [weight[:, i : i + 128] for i in range(0, own, 128)]
    pieces, rest = [], jnp.concatenate(lines, axis=0)
    for _ in range(SPLIT):
        piece = rest.astype(BF16).astype(F32)
        pieces.append(piece)
        rest = rest - piece
    rows = SPLIT * len(lines)
    pad = -rows % TILE
    pack_ref[own:, :] = jnp.concatenate(pieces + [jnp.zeros((pad, 128), F32)], axis=0).astype(BF16)
    acc[...] = jnp.zeros_like(acc)

    def step(at):
        code = code_ref[at, :]
        factor = 1.0 / (total * jnp.sum(code * token_scale, axis=1, keepdims=True))
        scaled = code * factor
        code_ref[at, :] = scaled
        acc[...] += sublane_sums(scaled)

    steps("middle", code_ref.shape[0], step)
    out_ref[...] = jnp.sum(acc[...], axis=0, keepdims=True)


def logit(centre, tok, code, token_scale, weight, scale):
    pred = jnp.exp2(similarity(centre, tok) * scale) * weight
    return (pred - code * token_scale).astype(BF16)


def token_half(code_ref, centre_ref, tok_ref, weight_ref, scale_ref, grad_ref, logit_ref, acc, *, scale, total, other):
    half = tok_ref.shape[0] // 2
    core = lax.rem(lax.axis_index("proto"), 2)
    at_half = part(1 - core if other else core, half)
    block = block_of("token", code_ref.shape[0])
    acc[...] = jnp.zeros_like(acc)

    def fill(i, slot, m):
        at = part(i, block)
        logit_ref[at, :] = logit(
            centre_ref[at, :],
            tok_ref[at_half, :],
            code_ref[at, at_half],
            scale_ref[:, at_half],
            weight_ref[:, at_half],
            scale,
        )

    def work(i, slot, m):
        at = part(i, block)
        acc[...] += lax.dot_general(
            centre_ref[at, :], logit_ref[at, :], (((0,), (0,)), ((), ())), preferred_element_type=F32
        )

    pipelined(code_ref.shape[0] // block, fill, work)
    grad_ref[...] = acc[...].T * total ** (-0.5)


def other_half(*refs, parts, scale, total):
    _, centre_ref, tok_ref, weight_ref = refs[:4]
    code_ref, grad_ref, logit_ref, scale_ref, acc = refs[4 + parts :]
    scale_ref[...] = total / term_sum(refs[4 : 4 + parts])
    token_half(
        code_ref, centre_ref, tok_ref, weight_ref, scale_ref, grad_ref, logit_ref, acc,
        scale=scale, total=total, other=True,
    )


def kept_half(_, centre_ref, tok_ref, weight_ref, scale_ref, code_ref, grad_ref, logit_ref, acc, *, scale, total):
    token_half(
        code_ref, centre_ref, tok_ref, weight_ref, scale_ref, grad_ref, logit_ref, acc,
        scale=scale, total=total, other=False,
    )


def proto_part(*refs, parts, scale):
    code_ref, centre_ref, tok_ref, scale_ref, kept_ref, other_ref = refs[:6]
    packs = refs[6 : 6 + parts]
    result_ref, tok, weight, out_ref, sems, *slots = refs[6 + parts :]
    tokens, own = code_ref.shape[1], tok_ref.shape[0]
    for i, pack in enumerate(packs):
        tok[i * own : (i + 1) * own, :] = pack[:own, :]
        pieces = pack[own:, :].astype(F32)
        count = own // 128
        lines = sum(pieces[j * count : (j + 1) * count, :] for j in range(SPLIT))
        for j in range(count):
            at = i * own + j * 128
            weight[:, at : at + 128] = lines[j : j + 1, :]

    subs = SUBS["proto"]
    size = code_ref.shape[0] // subs

    def fill(i, slot, m):
        at = part(i, CHUNK)
        c = pl.ds(pl.multiple_of(own + i * CHUNK, 128), CHUNK)
        r = slice(m * size, (m + 1) * size)
        slots[slot][r, :] = logit(
            centre_ref[r, :], tok[at, :], code_ref[r, c], scale_ref[:, c], weight[:, at], scale
        )

    def work(i, slot, m):
        r = slice(m * size, (m + 1) * size)
        out_ref[r, :] += jnp.dot(slots[slot][r, :], tok[part(i, CHUNK), :], preferred_element_type=F32)

    core = lax.rem(lax.axis_index("proto"), 2)
    out_ref[...] = sum(
        jnp.dot(ref[...], tok_ref[part(half, own // 2), :], preferred_element_type=F32)
        for ref, half in ((kept_ref, core), (other_ref, 1 - core))
    )
    count = parts * own // CHUNK
    copies = []

    def end():
        rows = out_ref.shape[0] // COPIES
        for j in range(COPIES):
            r = slice(j * rows, (j + 1) * rows)
            last = jnp.dot(slots[1][r, :], tok[part(count - 1, CHUNK), :], preferred_element_type=F32)
            out_ref[r, :] = (out_ref[r, :] + last) * tokens ** (-0.5)
            copies.append(
                pltpu.make_async_copy(out_ref.at[pl.ds(j * rows, rows)], result_ref.at[pl.ds(j * rows, rows)], sems.at[j])
            )
            copies[-1].start()

    pipelined(count, fill, work, subs, end)
    for c in copies:
        c.wait()


def swapped(x, axis, mask):
    return lax.ppermute(x, axis, [(i, i ^ mask) for i in range(lax.axis_size(axis))])


def others_of(x, axis):
    return [swapped(x, axis, m) for m in range(lax.axis_size(axis) - 1, 0, -1)]


def proto_terms(x):
    n = lax.axis_size("proto")
    x = x + swapped(x, "proto", 1)
    terms, unit = [x], 2
    while unit < n:
        group = min(4, n // unit)
        if unit > 2:
            terms = [sum(terms)]
        terms = [terms[0]] + [swapped(terms[0], "proto", unit * m) for m in range(group - 1, 0, -1)]
        unit *= group
    return terms


def chip_sum(x):
    n, unit = lax.axis_size("proto"), 2
    while unit < n:
        group = min(4, n // unit)
        x = sum([swapped(x, "proto", unit * m) for m in range(group - 1, 0, -1)], x)
        unit *= group
    return x


def local(first_view, alternate_augmentation, prototypes):
    own, d = first_view.shape
    k = prototypes.shape[0]
    tokens = own * lax.axis_size("dp")
    total = float(k * lax.axis_size("proto"))
    log2e = math.log2(math.e)
    code_scale = log2e / d / CODE_TEMP
    pred_scale = log2e / d / PRED_TEMP
    acc = pltpu.VMEM((8, tokens), F32)

    views = others_of(first_view, "dp")
    code, centres, columns = run(
        functools.partial(own_codes, scale=code_scale),
        [shape(k, tokens), shape(k, d, dtype=BF16), shape(k, 128)],
        [prototypes, first_view],
        [],
        keep=(0, 1, 2),
        us=3,
    )
    parts = len(views)
    code, columns = run(
        functools.partial(more_codes, scale=code_scale),
        [shape(k, 128)],
        [code, centres, columns, views[0]],
        [],
        resident=[1, 2, 3],
        keep=[0],
        thread=True,
        us=2,
    )
    views = views[1:]
    code, sums = run(
        functools.partial(first_pass, parts=len(views), scale=code_scale, total=total),
        [shape(1, tokens)],
        [code, centres, columns] + views,
        [pltpu.VMEM((len(views) * own, d), BF16), acc, pltpu.VMEM((k, 128), F32)],
        resident=list(range(1, 3 + len(views))),
        keep=[0],
        thread=True,
        us=7,
    )
    terms = proto_terms(sums)
    code, tok, den = run(
        functools.partial(denominators, scale=pred_scale),
        [shape(own, d, dtype=BF16), shape(1, own)],
        [code, centres, alternate_augmentation],
        [pltpu.VMEM((8, own), F32)],
        resident=[1],
        keep=[0, 1],
        thread=True,
        us=2,
    )
    code, sums = run(
        functools.partial(middle_pass, parts=len(terms), total=total),
        [shape(1, tokens + own)],
        [code] + terms + [den],
        [acc],
        resident=list(range(1, 2 + len(terms))),
        keep=[0],
        thread=True,
        us=5,
    )
    terms = proto_terms(sums)
    terms = terms[:1] + terms[2:] + terms[1:2]
    pack_rows = own + -(-SPLIT * own // 128 // TILE) * TILE
    code, sums, weight, pack = run(
        functools.partial(last_pass, parts=len(terms), total=total),
        [shape(1, tokens), shape(1, own), shape(pack_rows, d, dtype=BF16)],
        [code] + terms + [tok],
        [acc],
        resident=list(range(1, 2 + len(terms))),
        keep=[0, 1, 2],
        thread=True,
        us=5,
    )
    terms = proto_terms(sums)
    packs = others_of(pack, "dp")
    code, other, other_logits, token_scale = run(
        functools.partial(other_half, parts=len(terms), scale=pred_scale, total=total),
        [shape(own // 2, d), shape(k, own // 2, dtype=BF16), shape(1, tokens)],
        [code, centres, tok, weight] + terms,
        [pltpu.VMEM((d, own // 2), F32)],
        resident=list(range(1, 4 + len(terms))),
        keep=[0, 1, 2],
        thread=True,
        us=2,
    )
    code, mine, kept_logits = run(
        functools.partial(kept_half, scale=pred_scale, total=total),
        [shape(own // 2, d), shape(k, own // 2, dtype=BF16)],
        [code, centres, tok, weight, token_scale],
        [pltpu.VMEM((d, own // 2), F32)],
        resident=list(range(1, 5)),
        keep=[0, 1],
        thread=True,
        us=2,
    )
    mine = chip_sum(mine + swapped(other, "proto", 1))
    (proto_grad,) = run(
        functools.partial(proto_part, parts=parts, scale=pred_scale),
        [shape(k, d)],
        [code, centres, tok, token_scale, kept_logits, other_logits] + packs,
        [pltpu.VMEM((tokens - own, d), BF16), pltpu.VMEM((1, tokens - own), F32)]
        + [pltpu.VMEM((k, d), F32), pltpu.SemaphoreType.DMA((COPIES,))]
        + [pltpu.VMEM((k, CHUNK), BF16)] * 2,
        resident=range(6 + parts),
        copied=[0],
        us=10,
    )
    mine, proto_grad = lax.optimization_barrier((mine, proto_grad))
    other = swapped(mine, "proto", 1)
    first = lax.rem(lax.axis_index("proto"), 2) == 0
    token_grad = jnp.where(
        first, jnp.concatenate([mine, other]), jnp.concatenate([other, mine])
    )
    return proto_grad, token_grad


def solution(mesh):
    return jax.shard_map(
        local,
        mesh=mesh,
        in_specs=(P("dp", None), P("dp", None), P("proto", None)),
        out_specs=(P("proto", None), P("dp", None)),
        check_vma=False,
    )
```

```python
import functools
import math

import jax
import jax.numpy as jnp
from jax import lax
from jax.experimental import pallas as pl
from jax.experimental.pallas import tpu as pltpu
from jax.sharding import PartitionSpec as P

CODE_TEMP = 0.05
PRED_TEMP = 0.1
F32 = jnp.float32
BF16 = jnp.bfloat16
VMEM_LIMIT = 20 << 20
CHUNK = 256
BLOCKS = {"own": 2048, "first": 1024, "den": 2048, "middle": 512, "token": 2048}
SUBS = {"first": 1, "proto": 1}
COPIES = 4
SPLIT = 3
TILE = 16


def vmem_spec():
    return pl.BlockSpec(memory_space=pltpu.VMEM)


def shape(*dims, dtype=F32):
    return jax.ShapeDtypeStruct(dims, dtype)


def run(body, outs, args, scratch, resident=(), keep=(), us=1.0, thread=False, copied=()):
    if thread:
        outs = [shape(*args[0].shape, dtype=args[0].dtype)] + outs
        keep = [0] + [i + 1 for i in keep]
        resident = [0] + list(resident)
    return pl.pallas_call(
        body,
        out_shape=tuple(pltpu.VMEM(s.shape, s.dtype) if i in keep else s for i, s in enumerate(outs)),
        in_specs=[vmem_spec()] * len(args),
        out_specs=tuple(
            pl.BlockSpec(memory_space=pl.ANY) if i in copied else vmem_spec() for i in range(len(outs))
        ),
        scratch_shapes=scratch,
        input_output_aliases={0: 0} if thread else {},
        compiler_params=pltpu.CompilerParams(vmem_limit_bytes=VMEM_LIMIT),
        cost_estimate=pl.CostEstimate(flops=int(us * 1e9), bytes_accessed=1 << 20, transcendentals=0),
    )(
        *[
            pltpu.with_memory_space_constraint(a, pltpu.VMEM) if i in resident else a
            for i, a in enumerate(args)
        ]
    )


def normalize(values):
    floats = values.astype(F32)
    mean_square = jnp.mean(floats * floats, axis=-1, keepdims=True)
    return (floats * lax.rsqrt(mean_square + 1e-06)).astype(BF16)


def steps(name, size, step):
    block = min(BLOCKS[name], size)

    def body(i, carry):
        step(pl.ds(pl.multiple_of(i * block, block), block))
        return carry

    lax.fori_loop(0, size // block, body, 0)


def block_of(name, size):
    return min(BLOCKS[name], size // 2)


def pipelined(n, fill, work, subs=1, end=None):
    def both(i, slot):
        for m in range(subs):
            fill(i, slot, m)
            work(i - 1, 1 - slot, m)

    def body(i, carry):
        both(2 * i + 1, 1)
        both(2 * i + 2, 0)
        return carry

    for m in range(subs):
        fill(0, 0, m)
    if n <= 4:
        for i in range(1, n - 1):
            both(i, i % 2)
    else:
        lax.fori_loop(0, n // 2 - 1, body, 0)
    both(n - 1, 1)
    if end is not None:
        end()
    else:
        for m in range(subs):
            work(n - 1, 1, m)


def part(i, size):
    return pl.ds(i * size if isinstance(i, int) else pl.multiple_of(i * size, size), size)


def similarity(a, b):
    return lax.dot_general(a, b, (((1,), (1,)), ((), ())), preferred_element_type=F32)


def sublane_sums(block):
    return jnp.sum(block.reshape(block.shape[0] // 8, 8, block.shape[1]), axis=0)


def lane_sums(block):
    return sum(block[:, i : i + 128] for i in range(0, block.shape[1], 128))


def own_codes(proto_ref, token_ref, code_ref, centre_ref, column_ref, *, scale):
    own = token_ref.shape[0]
    tok = normalize(token_ref[...])

    def step(at):
        centre = normalize(proto_ref[at, :])
        centre_ref[at, :] = centre
        code = jnp.exp2(similarity(centre, tok) * scale)
        code_ref[at, :own] = code
        column_ref[at, :] = lane_sums(code)

    steps("own", proto_ref.shape[0], step)


def more_codes(_, centre_ref, column_ref, token_ref, code_ref, out_ref, *, scale):
    own = token_ref.shape[0]
    tok = normalize(token_ref[...])

    def step(at):
        code = jnp.exp2(similarity(centre_ref[at, :], tok) * scale)
        code_ref[at, own : 2 * own] = code
        out_ref[at, :] = column_ref[at, :] + lane_sums(code)

    steps("own", centre_ref.shape[0], step)


def first_pass(*refs, parts, scale, total):
    (_, centre_ref, column_ref), token_refs = refs[:3], refs[3 : 3 + parts]
    code_ref, out_ref, tok, acc, columns = refs[3 + parts :]
    n = token_refs[0].shape[0]
    done = code_ref.shape[1] - parts * n
    for i, t in enumerate(token_refs):
        tok[i * n : (i + 1) * n, :] = normalize(t[...])
    acc[...] = jnp.zeros_like(acc)
    block = block_of("first", centre_ref.shape[0])

    size = block // SUBS["first"]

    def rows(i, m):
        start = i * block + m * size
        return pl.ds(start if isinstance(i, int) else pl.multiple_of(start, size), size)

    def fill(i, slot, m):
        at = rows(i, m)
        code = jnp.exp2(similarity(centre_ref[at, :], tok[...]) * scale)
        code_ref[at, done:] = code
        columns[at, :] = column_ref[at, :] + lane_sums(code)

    def work(i, slot, m):
        at = rows(i, m)
        factor = 1.0 / (total * jnp.sum(columns[at, :], axis=1, keepdims=True))
        acc[...] += sublane_sums(code_ref[at, :] * factor)

    pipelined(centre_ref.shape[0] // block, fill, work, SUBS["first"])
    out_ref[...] = jnp.sum(acc[...], axis=0, keepdims=True)


def denominators(_, centre_ref, token_ref, code_ref, tok_ref, out_ref, acc, *, scale):
    tok_ref[...] = normalize(token_ref[...])
    acc[...] = jnp.zeros_like(acc)

    def step(at):
        acc[...] += sublane_sums(jnp.exp2(similarity(centre_ref[at, :], tok_ref[...]) * scale))

    steps("den", centre_ref.shape[0], step)
    out_ref[...] = jnp.sum(acc[...], axis=0, keepdims=True)


def term_sum(refs):
    return functools.reduce(lambda a, b: a + b, [r[...] for r in refs])


def middle_pass(*refs, parts, total):
    den_ref, (code_ref, out_ref, acc) = refs[1 + parts], refs[2 + parts :]
    token_scale = 1.0 / term_sum(refs[1 : 1 + parts])
    acc[...] = jnp.zeros_like(acc)

    def step(at):
        code = code_ref[at, :]
        factor = 1.0 / (total * jnp.sum(code * token_scale, axis=1, keepdims=True))
        acc[...] += sublane_sums(code * factor)

    steps("middle", code_ref.shape[0], step)
    tokens = acc.shape[1]
    out_ref[:, :tokens] = jnp.sum(acc[...], axis=0, keepdims=True)
    out_ref[:, tokens:] = den_ref[...]


def last_pass(*refs, parts, total):
    tok_ref, (code_ref, out_ref, weight_ref, pack_ref, acc) = refs[1 + parts], refs[2 + parts :]
    tokens, own = acc.shape[1], tok_ref.shape[0]
    sums = term_sum(refs[1 : 1 + parts])
    token_scale = 1.0 / sums[:, :tokens]
    weight = total / sums[:, tokens:]
    weight_ref[...] = weight
    pack_ref[:own, :] = tok_ref[...]
    lines = [weight[:, i : i + 128] for i in range(0, own, 128)]
    pieces, rest = [], jnp.concatenate(lines, axis=0)
    for _ in range(SPLIT):
        piece = rest.astype(BF16).astype(F32)
        pieces.append(piece)
        rest = rest - piece
    rows = SPLIT * len(lines)
    pad = -rows % TILE
    pack_ref[own:, :] = jnp.concatenate(pieces + [jnp.zeros((pad, 128), F32)], axis=0).astype(BF16)
    acc[...] = jnp.zeros_like(acc)

    def step(at):
        code = code_ref[at, :]
        factor = 1.0 / (total * jnp.sum(code * token_scale, axis=1, keepdims=True))
        scaled = code * factor
        code_ref[at, :] = scaled
        acc[...] += sublane_sums(scaled)

    steps("middle", code_ref.shape[0], step)
    out_ref[...] = jnp.sum(acc[...], axis=0, keepdims=True)


def logit(centre, tok, code, token_scale, weight, scale):
    pred = jnp.exp2(similarity(centre, tok) * scale) * weight
    return (pred - code * token_scale).astype(BF16)


def token_half(code_ref, centre_ref, tok_ref, weight_ref, scale_ref, grad_ref, logit_ref, acc, *, scale, total, other):
    half = tok_ref.shape[0] // 2
    core = lax.rem(lax.axis_index("proto"), 2)
    at_half = part(1 - core if other else core, half)
    block = block_of("token", code_ref.shape[0])
    acc[...] = jnp.zeros_like(acc)

    def fill(i, slot, m):
        at = part(i, block)
        logit_ref[at, :] = logit(
            centre_ref[at, :],
            tok_ref[at_half, :],
            code_ref[at, at_half],
            scale_ref[:, at_half],
            weight_ref[:, at_half],
            scale,
        )

    def work(i, slot, m):
        at = part(i, block)
        acc[...] += lax.dot_general(
            centre_ref[at, :], logit_ref[at, :], (((0,), (0,)), ((), ())), preferred_element_type=F32
        )

    pipelined(code_ref.shape[0] // block, fill, work)
    grad_ref[...] = acc[...].T * total ** (-0.5)


def other_half(*refs, parts, scale, total):
    _, centre_ref, tok_ref, weight_ref = refs[:4]
    code_ref, grad_ref, logit_ref, scale_ref, acc = refs[4 + parts :]
    scale_ref[...] = total / term_sum(refs[4 : 4 + parts])
    token_half(
        code_ref, centre_ref, tok_ref, weight_ref, scale_ref, grad_ref, logit_ref, acc,
        scale=scale, total=total, other=True,
    )


def kept_half(_, centre_ref, tok_ref, weight_ref, scale_ref, code_ref, grad_ref, logit_ref, acc, *, scale, total):
    token_half(
        code_ref, centre_ref, tok_ref, weight_ref, scale_ref, grad_ref, logit_ref, acc,
        scale=scale, total=total, other=False,
    )


def proto_part(*refs, parts, scale):
    code_ref, centre_ref, tok_ref, scale_ref, kept_ref, other_ref = refs[:6]
    packs = refs[6 : 6 + parts]
    result_ref, tok, weight, out_ref, sems, *slots = refs[6 + parts :]
    tokens, own = code_ref.shape[1], tok_ref.shape[0]
    for i, pack in enumerate(packs):
        tok[i * own : (i + 1) * own, :] = pack[:own, :]
        pieces = pack[own:, :].astype(F32)
        count = own // 128
        lines = sum(pieces[j * count : (j + 1) * count, :] for j in range(SPLIT))
        for j in range(count):
            at = i * own + j * 128
            weight[:, at : at + 128] = lines[j : j + 1, :]

    subs = SUBS["proto"]
    size = code_ref.shape[0] // subs

    def fill(i, slot, m):
        at = part(i, CHUNK)
        c = pl.ds(pl.multiple_of(own + i * CHUNK, 128), CHUNK)
        r = slice(m * size, (m + 1) * size)
        slots[slot][r, :] = logit(
            centre_ref[r, :], tok[at, :], code_ref[r, c], scale_ref[:, c], weight[:, at], scale
        )

    def work(i, slot, m):
        r = slice(m * size, (m + 1) * size)
        out_ref[r, :] += jnp.dot(slots[slot][r, :], tok[part(i, CHUNK), :], preferred_element_type=F32)

    core = lax.rem(lax.axis_index("proto"), 2)
    out_ref[...] = sum(
        jnp.dot(ref[...], tok_ref[part(half, own // 2), :], preferred_element_type=F32)
        for ref, half in ((kept_ref, core), (other_ref, 1 - core))
    )
    count = parts * own // CHUNK
    copies = []

    def end():
        rows = out_ref.shape[0] // COPIES
        for j in range(COPIES):
            r = slice(j * rows, (j + 1) * rows)
            last = jnp.dot(slots[1][r, :], tok[part(count - 1, CHUNK), :], preferred_element_type=F32)
            out_ref[r, :] = (out_ref[r, :] + last) * tokens ** (-0.5)
            copies.append(
                pltpu.make_async_copy(out_ref.at[pl.ds(j * rows, rows)], result_ref.at[pl.ds(j * rows, rows)], sems.at[j])
            )
            copies[-1].start()

    pipelined(count, fill, work, subs, end)
    for c in copies:
        c.wait()


def swapped(x, axis, mask):
    return lax.ppermute(x, axis, [(i, i ^ mask) for i in range(lax.axis_size(axis))])


def others_of(x, axis):
    return [swapped(x, axis, m) for m in range(lax.axis_size(axis) - 1, 0, -1)]


def proto_terms(x):
    n = lax.axis_size("proto")
    x = x + swapped(x, "proto", 1)
    terms, unit = [x], 2
    while unit < n:
        group = min(4, n // unit)
        if unit > 2:
            terms = [sum(terms)]
        terms = [terms[0]] + [swapped(terms[0], "proto", unit * m) for m in range(group - 1, 0, -1)]
        unit *= group
    return terms


def chip_sum(x):
    n, unit = lax.axis_size("proto"), 2
    while unit < n:
        group = min(4, n // unit)
        x = sum([swapped(x, "proto", unit * m) for m in range(group - 1, 0, -1)], x)
        unit *= group
    return x


def local(first_view, alternate_augmentation, prototypes):
    own, d = first_view.shape
    k = prototypes.shape[0]
    tokens = own * lax.axis_size("dp")
    total = float(k * lax.axis_size("proto"))
    log2e = math.log2(math.e)
    code_scale = log2e / d / CODE_TEMP
    pred_scale = log2e / d / PRED_TEMP
    acc = pltpu.VMEM((8, tokens), F32)

    views = others_of(first_view, "dp")
    code, centres, columns = run(
        functools.partial(own_codes, scale=code_scale),
        [shape(k, tokens), shape(k, d, dtype=BF16), shape(k, 128)],
        [prototypes, first_view],
        [],
        keep=(0, 1, 2),
        us=3,
    )
    parts = len(views)
    code, columns = run(
        functools.partial(more_codes, scale=code_scale),
        [shape(k, 128)],
        [code, centres, columns, views[0]],
        [],
        resident=[1, 2, 3],
        keep=[0],
        thread=True,
        us=2,
    )
    views = views[1:]
    code, tok, den = run(
        functools.partial(denominators, scale=pred_scale),
        [shape(own, d, dtype=BF16), shape(1, own)],
        [code, centres, alternate_augmentation],
        [pltpu.VMEM((8, own), F32)],
        resident=[1],
        keep=[0, 1],
        thread=True,
        us=2,
    )
    code, sums = run(
        functools.partial(first_pass, parts=len(views), scale=code_scale, total=total),
        [shape(1, tokens)],
        [code, centres, columns] + views,
        [pltpu.VMEM((len(views) * own, d), BF16), acc, pltpu.VMEM((k, 128), F32)],
        resident=list(range(1, 3 + len(views))),
        keep=[0],
        thread=True,
        us=7,
    )
    terms = proto_terms(sums)
    code, sums = run(
        functools.partial(middle_pass, parts=len(terms), total=total),
        [shape(1, tokens + own)],
        [code] + terms + [den],
        [acc],
        resident=list(range(1, 2 + len(terms))),
        keep=[0],
        thread=True,
        us=5,
    )
    terms = proto_terms(sums)
    terms = terms[:1] + terms[2:] + terms[1:2]
    pack_rows = own + -(-SPLIT * own // 128 // TILE) * TILE
    code, sums, weight, pack = run(
        functools.partial(last_pass, parts=len(terms), total=total),
        [shape(1, tokens), shape(1, own), shape(pack_rows, d, dtype=BF16)],
        [code] + terms + [tok],
        [acc],
        resident=list(range(1, 2 + len(terms))),
        keep=[0, 1, 2],
        thread=True,
        us=5,
    )
    terms = proto_terms(sums)
    packs = others_of(pack, "dp")
    code, other, other_logits, token_scale = run(
        functools.partial(other_half, parts=len(terms), scale=pred_scale, total=total),
        [shape(own // 2, d), shape(k, own // 2, dtype=BF16), shape(1, tokens)],
        [code, centres, tok, weight] + terms,
        [pltpu.VMEM((d, own // 2), F32)],
        resident=list(range(1, 4 + len(terms))),
        keep=[0, 1, 2],
        thread=True,
        us=2,
    )
    code, mine, kept_logits = run(
        functools.partial(kept_half, scale=pred_scale, total=total),
        [shape(own // 2, d), shape(k, own // 2, dtype=BF16)],
        [code, centres, tok, weight, token_scale],
        [pltpu.VMEM((d, own // 2), F32)],
        resident=list(range(1, 5)),
        keep=[0, 1],
        thread=True,
        us=2,
    )
    mine = chip_sum(mine + swapped(other, "proto", 1))
    (proto_grad,) = run(
        functools.partial(proto_part, parts=parts, scale=pred_scale),
        [shape(k, d)],
        [code, centres, tok, token_scale, kept_logits, other_logits] + packs,
        [pltpu.VMEM((tokens - own, d), BF16), pltpu.VMEM((1, tokens - own), F32)]
        + [pltpu.VMEM((k, d), F32), pltpu.SemaphoreType.DMA((COPIES,))]
        + [pltpu.VMEM((k, CHUNK), BF16)] * 2,
        resident=range(6 + parts),
        copied=[0],
        us=10,
    )
    mine, proto_grad = lax.optimization_barrier((mine, proto_grad))
    other = swapped(mine, "proto", 1)
    first = lax.rem(lax.axis_index("proto"), 2) == 0
    token_grad = jnp.where(
        first, jnp.concatenate([mine, other]), jnp.concatenate([other, mine])
    )
    return proto_grad, token_grad


def solution(mesh):
    return jax.shard_map(
        local,
        mesh=mesh,
        in_specs=(P("dp", None), P("dp", None), P("proto", None)),
        out_specs=(P("proto", None), P("dp", None)),
        check_vma=False,
    )
```
